32 devices in a mesh: row: 16 (over z, x, core), col: 2 (over y).
Axes of the slice: x: 2, y: 2, z: 4, core: 2. Of those that a mesh axis runs over, the one named last changes fastest.
Arguments:
- features: bfloat16 [128, 64, 384], P('row', 'col'), may hold values from -6 to 6
- depth_weight: float32 [7, 7, 384], replicated, may hold values from -0.875 to 0.875
- depth_bias: float32 [384], replicated, may hold values from -3 to 3
- norm_gain: float32 [384], replicated, may hold values from 0.25 to 1.75
- norm_bias: float32 [384], replicated, may hold values from -2 to 2
- expand_weight: bfloat16 [384, 1536], replicated, may hold values from -0.3125 to 0.3125
- expand_bias: float32 [1536], replicated, may hold values from -3 to 3
- shrink_weight: bfloat16 [1536, 384], replicated, may hold values from -0.15625 to 0.15625
- shrink_bias: float32 [384], replicated, may hold values from -3 to 3
- layer_scale: float32 [384], replicated, may hold values from 0.3 to 3
- key_weight: bfloat16 [384, 384], replicated, may hold values from -0.3125 to 0.3125
- value_weight: bfloat16 [384, 384], replicated, may hold values from -0.3125 to 0.3125
- queries: bfloat16 [64, 384], replicated, may hold values from -192 to 192
- class_weight: float32 [384, 16], replicated, may hold values from -0.109375 to 0.109375
- tissue: int32 [16, 8], P('row', 'col'), may hold values from 0 to 1, as said below
- slide_label: int32 [16], replicated, may hold values from 0 to 1
Outputs:
- block_out: bfloat16 [128, 64, 384], P('row', 'col')
- pooled: float32 [64, 384], replicated
- slide_loss: float32 [1], replicated
The draws below stay inside these ranges and needn't reach their ends.
Inputs may be any that keep to these rules, and one draw needn't show every extreme that they name: 0 or 1; tissue[0, 0] is 1.
All inputs are finite; a program needn't handle non-finite values.
Results may differ from the reference program's by a relative error of at most 0.028.
The reference program's roundings to bfloat16 on the way (of `normed`, `hidden` and `rounded`) count: a program that leaves them out, or rounds other values in their place, can miss the bound.
Values may be sent and summed in bfloat16 or wider, within the bound.
A program may use at most 128 MiB of HBM per device.

```python
import math
import jax
import jax.numpy as jnp
from jax import lax

C = 384
HID = 1536
NH = 8
NQ = 64
NLAB = 16
TILE = 8
CH = 8
HT = 128
WT = 64
NTR = 16
NTC = 8
N_ROW = 16


def draw_tissue(key, part):
    rolls = jax.random.randint(key, (NTR, NTC), 0, 100)
    bands = jnp.arange(NTR, dtype=jnp.int32)[:, None]
    limits = 20 + 70 * bands // NTR
    drawn = (rolls < limits).astype(jnp.int32)
    return drawn.at[0, 0].set(1)


def draw_queries(key, part):
    key_order = jax.random.fold_in(key, 11)
    key_entry = jax.random.fold_in(key, 12)
    order = jax.random.permutation(key_order, NQ).astype(jnp.float32)
    gains = jnp.exp(order * (jnp.log(48.0) / (NQ - 1)))
    entries = jnp.clip(jax.random.normal(key_entry, (NQ, C), jnp.float32), -4.0, 4.0)
    return (entries * gains[:, None]).astype(jnp.bfloat16)


def set_ends(values, stream_key, least, top_value):
    extent = values.shape
    place = [jax.random.randint(jax.random.fold_in(stream_key, axis), (), 0, extent[axis]) for axis in range(len(extent))]
    values = values.at[tuple(place)].set(least)
    longest = extent.index(max(extent))
    place[longest] = (place[longest] + 1) % extent[longest]
    return values.at[tuple(place)].set(top_value)


def block_levels(stream_key, extent, split, low, high):
    level, own = 1.0, jax.random.fold_in(stream_key, 6)
    for dim, parts in split:
        draws = jnp.exp(jax.random.uniform(jax.random.fold_in(own, dim), (parts,), jnp.float32, low / len(split), high / len(split)))
        level = level * jnp.repeat(draws, extent[dim] // parts).reshape([-1 if axis == dim else 1 for axis in range(len(extent))])
    return level


def bell_draw(rng, dims, spread, reach, cuts=(), held_as=jnp.bfloat16):
    level = block_levels(rng, dims, cuts, -0.22, 0.18) if cuts else 1.0
    result = jax.random.normal(rng, dims, jnp.float32) * spread * level
    return jnp.minimum(jnp.maximum(result, -reach), reach).astype(held_as)


def setup_inputs(seed: int = 0) -> dict:
    arg_keys = jax.random.split(jax.random.key(seed), 17)
    return {
        "features": bell_draw(arg_keys[0], (HT, WT, C), 1.0, 6.0, ((0, 16), (1, 2))),
        "depth_weight": bell_draw(arg_keys[1], (7, 7, C), 49 ** -0.5, 0.875, (), jnp.float32),
        "depth_bias": bell_draw(arg_keys[2], (C,), 0.5, 3.0, (), jnp.float32),
        "norm_gain": jnp.clip(1.0 + 0.15 * jax.random.normal(arg_keys[3], (C,), jnp.float32), 0.25, 1.75),
        "norm_bias": bell_draw(arg_keys[4], (C,), 0.3, 2.0, (), jnp.float32),
        "expand_weight": bell_draw(arg_keys[5], (C, HID), C ** -0.5, 0.3125),
        "expand_bias": bell_draw(arg_keys[6], (HID,), 0.5, 3.0, (), jnp.float32),
        "shrink_weight": bell_draw(arg_keys[7], (HID, C), HID ** -0.5, 0.15625),
        "shrink_bias": bell_draw(arg_keys[8], (C,), 0.5, 3.0, (), jnp.float32),
        "layer_scale": jnp.clip(jnp.exp(jax.random.uniform(arg_keys[9], (C,), jnp.float32, math.log(0.3), math.log(3.0))), 0.3, 3.0),
        "key_weight": bell_draw(arg_keys[10], (C, C), C ** -0.5, 0.3125),
        "value_weight": bell_draw(arg_keys[11], (C, C), C ** -0.5, 0.3125),
        "queries": draw_queries(jax.random.fold_in(arg_keys[16], 71), 0),
        "class_weight": bell_draw(arg_keys[13], (C, NLAB), (NQ * C // 8) ** -0.5, 0.109375, (), jnp.float32),
        "tissue": draw_tissue(jax.random.fold_in(arg_keys[16], 71), 0),
        "slide_label": set_ends(jax.random.randint(arg_keys[15], (NLAB,), 0, 2), jax.random.fold_in(arg_keys[15], 1), 0, 1).astype(jnp.int32),
    }


def spread_heads(scale, width):
    return jnp.repeat(jnp.transpose(scale), width // scale.shape[0], axis=1)

def band_work(band, padded, features, tissue, depth_weight, depth_bias, norm_gain, norm_bias, expand_weight, expand_bias, shrink_weight, shrink_bias, layer_scale, key_weight, value_weight, queries):
    start = (band * CH).astype(jnp.int32)
    window = lax.dynamic_slice_in_dim(padded, start, CH + 6, 0)
    conv = jnp.zeros((CH, WT, C), jnp.float32) + depth_bias
    for offset_row in range(7):
        for offset_col in range(7):
            conv = conv + window[offset_row:offset_row + CH, offset_col:offset_col + WT].astype(jnp.float32) * depth_weight[offset_row, offset_col]
    center = lax.optimization_barrier(jnp.mean(conv, axis=-1, keepdims=True))
    variance = lax.optimization_barrier(jnp.mean((conv - center) ** 2, axis=-1, keepdims=True))
    normed = ((conv - center) * lax.rsqrt(variance + 1e-06) * norm_gain + norm_bias).astype(jnp.bfloat16)
    expanded = jnp.dot(normed.reshape(CH * WT, C), expand_weight, preferred_element_type=jnp.float32) + expand_bias
    hidden = jax.nn.gelu(expanded, approximate=False).astype(jnp.bfloat16)
    shrunk = jnp.dot(hidden, shrink_weight, preferred_element_type=jnp.float32) + shrink_bias
    inputs = lax.dynamic_slice_in_dim(features, start, CH, 0).reshape(CH * WT, C)
    block_out = (inputs.astype(jnp.float32) + layer_scale * shrunk).astype(jnp.bfloat16)
    keys = jnp.dot(block_out, key_weight, preferred_element_type=jnp.float32).astype(jnp.bfloat16)
    values = jnp.dot(block_out, value_weight, preferred_element_type=jnp.float32).astype(jnp.bfloat16)
    tile_rows = lax.dynamic_slice_in_dim(tissue, (band * (CH // TILE)).astype(jnp.int32), CH // TILE, 0)
    live_cells = jnp.repeat(jnp.repeat(tile_rows, TILE, axis=0), TILE, axis=1).reshape(CH * WT) > 0
    size = C // NH
    query_heads = queries.astype(jnp.float32).reshape(NQ, NH, size)
    key_heads = keys.astype(jnp.float32).reshape(CH * WT, NH, size)
    scores = jnp.einsum('qhd,nhd->hqn', query_heads, key_heads) * size ** (-0.5)
    live = live_cells[None, None, :]
    scores = jnp.where(live, scores, -1e+30)
    peak = lax.optimization_barrier(jnp.max(scores, axis=2))
    weights = jnp.where(live, jnp.exp(scores - peak[:, :, None]), 0.0)
    total = lax.optimization_barrier(jnp.sum(weights, axis=2))
    rounded = weights.astype(jnp.bfloat16)
    weighted = jnp.einsum('hqn,nhd->qhd', rounded.astype(jnp.float32), values.astype(jnp.float32).reshape(CH * WT, NH, size)).reshape(NQ, C)
    return (block_out.reshape(CH, WT, C), peak, total, weighted)

def reference(features, depth_weight, depth_bias, norm_gain, norm_bias, expand_weight, expand_bias, shrink_weight, shrink_bias, layer_scale, key_weight, value_weight, queries, class_weight, tissue, slide_label):
    padded = jnp.pad(features, ((3, 3), (3, 3), (0, 0)))

    def one_band(band):
        return band_work(band, padded, features, tissue, depth_weight, depth_bias, norm_gain, norm_bias, expand_weight, expand_bias, shrink_weight, shrink_bias, layer_scale, key_weight, value_weight, queries)
    bands, peaks, totals, weighted = lax.map(one_band, jnp.arange(N_ROW, dtype=jnp.int32))
    block_out = bands.reshape(HT, WT, C)
    peak = lax.optimization_barrier(jnp.max(peaks, axis=0))
    factors = jnp.exp(peaks - peak[None])
    total = lax.optimization_barrier(jnp.sum(totals * factors, axis=0))
    summed = jnp.zeros((NQ, C), jnp.float32)
    for band in range(N_ROW):
        summed = summed + weighted[band] * spread_heads(factors[band], C)
    pooled = summed / spread_heads(total, C)
    logits = lax.optimization_barrier(jnp.sum(jnp.dot(pooled, class_weight, precision=lax.Precision.HIGHEST), axis=0))
    slide_loss = jnp.sum(jax.nn.softplus(logits) - slide_label.astype(jnp.float32) * logits).reshape(1)
    return (block_out, pooled, slide_loss)
```

```python
import functools

import jax
import jax.numpy as jnp
from jax import lax
from jax.experimental import pallas as pl
from jax.experimental.pallas import tpu as pltpu
from jax.sharding import PartitionSpec as P

NH = 8
NQ = 64
TILE = 8
LANES = 128
GROUP_ROWS, GROUP_COLS = 4, 2
GROUP = GROUP_ROWS * GROUP_COLS
QROWS = NQ // GROUP
MESH = pl.DeviceIdType.MESH
SIDES = [(-1, 0), (1, 0), (0, -1), (0, 1), (-1, -1), (-1, 1), (1, -1), (1, 1)]


def lane_ids(rows, width):
    return lax.broadcasted_iota(jnp.int32, (rows, width), 1)


def spread(cols, first, width):
    rows = cols.shape[0]
    head = lane_ids(rows, width) // (width // NH)
    out = jnp.zeros((rows, width), jnp.float32)
    for h in range(NH):
        out = jnp.where(head == h, cols[:, first + h : first + h + 1], out)
    return out


def combine(ref, count, width):
    tails = [ref[s, :, width:] for s in range(count)]
    peak = functools.reduce(jnp.maximum, tails)
    weighted = jnp.zeros((QROWS, width), jnp.float32)
    total = jnp.zeros((QROWS, LANES), jnp.float32)
    for s in range(count):
        factor = jnp.exp(tails[s] - peak)
        total = total + pltpu.roll(factor, NH, 1) * tails[s]
        weighted = weighted + ref[s, :, :width] * spread(factor, 0, width)
    return weighted, jnp.where(lane_ids(QROWS, LANES) < NH, peak, total)


def kernel(
    n_row, n_col,
    feat, dw, db, gain, nbias, w1_hbm, b1, w2_hbm, b2, scale, wk_hbm, wv_hbm, queries, cw, tissue, label,
    block_ref, pooled_ref, loss_ref,
    w1, w2, wk, wv, pad, left_pad, right_pad, conv, qbig,
    stage_l, stage_r, halo_rows, halo_cols, halo_corners, msg, got_a, got_b, mine, pooled,
    w_sem, hs_sem, hr_sem, as_sem, ar_sem, bs_sem, br_sem, cs_sem, cr_sem,
):
    rows, cols, width = feat.shape
    count = rows * cols
    chunks = width // LANES
    row, col = lax.axis_index("row"), lax.axis_index("col")

    loads = [
        pltpu.make_async_copy(src, dst, w_sem.at[i])
        for i, (src, dst) in enumerate(((w1_hbm, w1), (w2_hbm, w2), (wk_hbm, wk), (wv_hbm, wv)))
    ]
    for load in loads:
        load.start()

    base_row, base_col = (row // GROUP_ROWS) * GROUP_ROWS, (col // GROUP_COLS) * GROUP_COLS
    place = (row - base_row) * GROUP_COLS + (col - base_col)
    over = n_col // GROUP_COLS
    n_far = (n_row // GROUP_ROWS) * over
    far = (row // GROUP_ROWS) * over + col // GROUP_COLS

    def near_peer(step):
        other = (place + step) % GROUP
        return other, (base_row + other // GROUP_COLS, base_col + other % GROUP_COLS)

    def far_peer(step):
        other = (far + step) % n_far
        return other, (
            (other // over) * GROUP_ROWS + place // GROUP_COLS,
            (other % over) * GROUP_COLS + place % GROUP_COLS,
        )

    def present(side):
        dr, dc = side
        ok = None
        for delta, at, size in ((dr, row, n_row), (dc, col, n_col)):
            if delta:
                here = at > 0 if delta < 0 else at < size - 1
                ok = here if ok is None else jnp.logical_and(ok, here)
        return ok

    barrier = pltpu.get_barrier_semaphore()
    for side in SIDES:
        @pl.when(present(side))
        def _(side=side):
            pl.semaphore_signal(
                barrier, inc=1, device_id=(row + side[0], col + side[1]), device_id_type=MESH
            )
    for step in range(1, GROUP):
        pl.semaphore_signal(barrier, inc=1, device_id=near_peer(step)[1], device_id_type=MESH)
    for step in range(1, n_far):
        pl.semaphore_signal(barrier, inc=1, device_id=far_peer(step)[1], device_id_type=MESH)

    stage_l[...] = feat[:, 0:8, :].astype(jnp.float32).reshape(rows * 8, width).astype(jnp.bfloat16)
    stage_r[...] = (
        feat[:, cols - 8 : cols, :].astype(jnp.float32).reshape(rows * 8, width).astype(jnp.bfloat16)
    )

    landing = {
        (-1, 0): halo_rows.at[0], (1, 0): halo_rows.at[1],
        (0, -1): halo_cols.at[0], (0, 1): halo_cols.at[1],
        (-1, -1): halo_corners.at[0], (-1, 1): halo_corners.at[1],
        (1, -1): halo_corners.at[2], (1, 1): halo_corners.at[3],
    }

    def halo_copy(side):
        dr, dc = side
        if dc == 0:
            src = feat.at[pl.ds(0, 3)] if dr < 0 else feat.at[pl.ds(rows - 3, 3)]
        else:
            src = stage_l if dc < 0 else stage_r
            if dr:
                src = src.at[pl.ds(0 if dr < 0 else rows * 8 - 32, 32)]
        return pltpu.make_async_remote_copy(
            src_ref=src,
            dst_ref=landing[(-dr, -dc)],
            send_sem=hs_sem.at[SIDES.index(side)],
            recv_sem=hr_sem.at[SIDES.index((-dr, -dc))],
            device_id=(row + dr, col + dc),
            device_id_type=MESH,
        )

    greeted = jnp.int32(GROUP - 1 + n_far - 1)
    for side in SIDES:
        greeted = greeted + present(side).astype(jnp.int32)
    pl.semaphore_wait(barrier, greeted)
    for side in SIDES:
        @pl.when(present(side))
        def _(side=side):
            halo_copy(side).start()

        @pl.when(jnp.logical_not(present(side)))
        def _(side=side):
            landing[side][...] = jnp.zeros(landing[side].shape, jnp.bfloat16)

    for c in range(chunks):
        lanes = slice(c * LANES, (c + 1) * LANES)
        pad[c, 3 : 3 + rows, 8 : 8 + cols, :] = feat[:, :, lanes].astype(jnp.float32)
    pad[:, 3 : 3 + rows, 0:8, :] = jnp.zeros((chunks, rows, 8, LANES), jnp.float32)
    pad[:, 3 : 3 + rows, 8 + cols :, :] = jnp.zeros((chunks, rows, 8, LANES), jnp.float32)

    def own_part(c, carry):
        at = pl.ds(pl.multiple_of(c * LANES, LANES), LANES)
        acc = [jnp.broadcast_to(db[:, at], (cols, LANES)) for _ in range(rows)]
        for b in range(7):
            taps = [dw[a, b : b + 1, at] for a in range(7)]
            for r in range(3, 3 + rows):
                window = pad[c, r, b + 5 : b + 5 + cols, :]
                for a in range(7):
                    if 0 <= r - a < rows:
                        acc[r - a] = acc[r - a] + window * taps[a]
        for i in range(rows):
            conv[c, i] = acc[i]
        return carry

    lax.fori_loop(0, chunks, own_part, 0)

    q32 = queries[...].astype(jnp.float32)
    head = lane_ids(NQ, width) // (width // NH)
    for h in range(NH):
        qbig[h * NQ : (h + 1) * NQ, :] = jnp.where(head == h, q32, 0.0).astype(jnp.bfloat16)

    for side in SIDES:
        @pl.when(present(side))
        def _(side=side):
            pltpu.make_async_remote_copy(
                src_ref=landing[side],
                dst_ref=landing[side],
                send_sem=hs_sem.at[SIDES.index(side)],
                recv_sem=hr_sem.at[SIDES.index(side)],
                device_id=(row + side[0], col + side[1]),
                device_id_type=MESH,
            ).wait_recv()

    for c in range(chunks):
        lanes = slice(c * LANES, (c + 1) * LANES)
        for end, first in ((0, 0), (1, 3 + rows)):
            pad[c, first : first + 3, 8 : 8 + cols, :] = halo_rows[end, :, :, lanes].astype(jnp.float32)
            for side in range(2):
                corner = halo_corners[end * 2 + side, :, lanes].astype(jnp.float32).reshape(4, 8, LANES)
                start = 0 if side == 0 else 8 + cols
                pad[c, first : first + 3, start : start + 8, :] = corner[1:4] if end == 0 else corner[0:3]
        left_pad[c, :, 0:8, :] = halo_cols[0, :, lanes].astype(jnp.float32).reshape(rows, 8, LANES)
        right_pad[c, :, 8:16, :] = halo_cols[1, :, lanes].astype(jnp.float32).reshape(rows, 8, LANES)
    left_pad[:, :, 8:16, :] = jnp.zeros((chunks, rows, 8, LANES), jnp.float32)
    right_pad[:, :, 0:8, :] = jnp.zeros((chunks, rows, 8, LANES), jnp.float32)

    def border_part(c, carry):
        at = pl.ds(pl.multiple_of(c * LANES, LANES), LANES)
        acc = [conv[c, i] for i in range(rows)]
        low = [jnp.zeros((8, LANES), jnp.float32) for _ in range(rows)]
        high = [jnp.zeros((8, LANES), jnp.float32) for _ in range(rows)]
        for b in range(7):
            taps = [dw[a, b : b + 1, at] for a in range(7)]
            for r in list(range(3)) + list(range(3 + rows, 6 + rows)):
                window = pad[c, r, b + 5 : b + 5 + cols, :]
                for a in range(7):
                    if 0 <= r - a < rows:
                        acc[r - a] = acc[r - a] + window * taps[a]
            if b != 3:
                side, edge, start = (low, left_pad, b + 5) if b < 3 else (high, right_pad, b - 3)
                for r in range(3, 3 + rows):
                    window = edge[c, r - 3, start : start + 8, :]
                    for a in range(7):
                        if 0 <= r - a < rows:
                            side[r - a] = side[r - a] + window * taps[a]
        for i in range(rows):
            conv[c, i] = acc[i]
            conv[c, i, 0:8, :] = conv[c, i, 0:8, :] + low[i]
            conv[c, i, cols - 8 : cols, :] = conv[c, i, cols - 8 : cols, :] + high[i]
        return carry

    lax.fori_loop(0, chunks, border_part, 0)

    full = jnp.concatenate([conv[c].reshape(count, LANES) for c in range(chunks)], axis=1)
    center = jnp.mean(full, axis=-1, keepdims=True)
    off = full - center
    variance = jnp.mean(off * off, axis=-1, keepdims=True)
    normed = (off * lax.rsqrt(variance + 1e-06) * gain[...] + nbias[...]).astype(jnp.bfloat16)

    loads[0].wait()
    loads[1].wait()
    hid = w1.shape[1]
    piece = 384
    shrunk = jnp.zeros((count, width), jnp.float32)
    for start in range(0, hid, piece):
        part = slice(start, start + piece)
        expanded = jnp.dot(normed, w1[:, part], preferred_element_type=jnp.float32) + b1[:, part]
        hidden = (0.5 * expanded * (1.0 + lax.erf(expanded * 0.5**0.5))).astype(jnp.bfloat16)
        shrunk = shrunk + jnp.dot(hidden, w2[part, :], preferred_element_type=jnp.float32)
    shrunk = shrunk + b2[...]
    inputs = feat[...].astype(jnp.float32).reshape(count, width)
    block = (inputs + scale[...] * shrunk).astype(jnp.bfloat16)
    block_ref[...] = block.reshape(rows, cols, width)

    loads[2].wait()
    loads[3].wait()
    keys = jnp.dot(block, wk[...], preferred_element_type=jnp.float32).astype(jnp.bfloat16)
    values = jnp.dot(block, wv[...], preferred_element_type=jnp.float32).astype(jnp.bfloat16)
    scores = lax.dot_general(
        qbig[...], keys, (((1,), (1,)), ((), ())), preferred_element_type=jnp.float32
    ) * (width // NH) ** (-0.5)
    cell = lane_ids(1, count)
    tile = (cell // cols) // TILE * (cols // TILE) + (cell % cols) // TILE
    alive = jnp.zeros((1, count), jnp.int32)
    for i in range(rows // TILE):
        for j in range(cols // TILE):
            alive = jnp.where(tile == i * (cols // TILE) + j, tissue[i, j], alive)
    live = alive > 0
    scores = jnp.where(live, scores, -1e30)
    peak = jnp.max(scores, axis=1, keepdims=True)
    weights = jnp.where(live, jnp.exp(scores - peak), 0.0)
    total = jnp.sum(weights, axis=1, keepdims=True)
    mixed = jnp.dot(weights.astype(jnp.bfloat16), values, preferred_element_type=jnp.float32)
    weighted = jnp.zeros((NQ, width), jnp.float32)
    tail = jnp.zeros((NQ, LANES), jnp.float32)
    lane = lane_ids(NQ, LANES)
    for h in range(NH):
        own = slice(h * NQ, (h + 1) * NQ)
        weighted = jnp.where(head == h, mixed[own], weighted)
        tail = jnp.where(lane == h, peak[own], tail)
        tail = jnp.where(lane == NH + h, total[own], tail)
    msg[:, :width] = weighted
    msg[:, width:] = tail

    copies_a = []
    for step in range(1, GROUP):
        other, device = near_peer(step)
        copies_a.append((other, pltpu.make_async_remote_copy(
            src_ref=msg.at[pl.ds(pl.multiple_of(other * QROWS, QROWS), QROWS)],
            dst_ref=got_a.at[place],
            send_sem=as_sem.at[step],
            recv_sem=ar_sem.at[place],
            device_id=device,
            device_id_type=MESH,
        )))
        copies_a[-1][1].start()
    got_a[place] = msg[pl.ds(pl.multiple_of(place * QROWS, QROWS), QROWS), :]

    def arrival(dst, sem):
        return pltpu.make_async_remote_copy(
            src_ref=dst, dst_ref=dst, send_sem=as_sem.at[0], recv_sem=sem,
            device_id=near_peer(1)[1], device_id_type=MESH,
        )

    for step in range(1, GROUP):
        other = near_peer(step)[0]
        arrival(got_a.at[other], ar_sem.at[other]).wait_recv()
    weighted, tail = combine(got_a, GROUP, width)

    if n_far > 1:
        mine[:, :width] = weighted
        mine[:, width:] = tail
        copies_b = []
        for step in range(1, n_far):
            other, device = far_peer(step)
            copies_b.append(pltpu.make_async_remote_copy(
                src_ref=mine,
                dst_ref=got_b.at[far],
                send_sem=bs_sem.at[step],
                recv_sem=br_sem.at[far],
                device_id=device,
                device_id_type=MESH,
            ))
            copies_b[-1].start()
        got_b[far] = mine[...]
        for step in range(1, n_far):
            other = far_peer(step)[0]
            arrival(got_b.at[other], br_sem.at[other]).wait_recv()
        weighted, tail = combine(got_b, n_far, width)
    pooled[place] = weighted / spread(tail, NH, width)

    copies_c = []
    for step in range(1, GROUP):
        other, device = near_peer(step)
        copies_c.append(pltpu.make_async_remote_copy(
            src_ref=pooled.at[place],
            dst_ref=pooled.at[place],
            send_sem=cs_sem.at[step],
            recv_sem=cr_sem.at[place],
            device_id=device,
            device_id_type=MESH,
        ))
        copies_c[-1].start()
    for step in range(1, GROUP):
        other = near_peer(step)[0]
        arrival(pooled.at[other], cr_sem.at[other]).wait_recv()
    result = pooled[...].reshape(NQ, width)
    pooled_ref[...] = result
    summed = jnp.sum(result, axis=0, keepdims=True)
    logits = jnp.dot(
        jnp.broadcast_to(summed, (8, width)), cw[...],
        precision=lax.Precision.HIGHEST, preferred_element_type=jnp.float32,
    )[0:1]
    soft = jnp.maximum(logits, 0.0) + jnp.log1p(jnp.exp(-jnp.abs(logits)))
    loss_ref[0] = jnp.sum(soft - label[...].astype(jnp.float32) * logits)

    for side in SIDES:
        @pl.when(present(side))
        def _(side=side):
            halo_copy(side).wait_send()
    for _, copy in copies_a:
        copy.wait_send()
    if n_far > 1:
        for copy in copies_b:
            copy.wait_send()
    for copy in copies_c:
        copy.wait_send()


def per_device(
    n_row, n_col,
    features, depth_weight, depth_bias, norm_gain, norm_bias, expand_weight, expand_bias,
    shrink_weight, shrink_bias, layer_scale, key_weight, value_weight, queries, class_weight,
    tissue, slide_label,
):
    rows, cols, width = features.shape
    hid = expand_weight.shape[1]
    chunks = width // LANES
    n_far = (n_row // GROUP_ROWS) * (n_col // GROUP_COLS)
    vmem = pl.BlockSpec(memory_space=pltpu.VMEM)
    smem = pl.BlockSpec(memory_space=pltpu.SMEM)
    hbm = pl.BlockSpec(memory_space=pl.ANY)
    wide = width + LANES
    f32, bf16 = jnp.float32, jnp.bfloat16
    dma = pltpu.SemaphoreType.DMA
    block, pooled, loss = pl.pallas_call(
        functools.partial(kernel, n_row, n_col),
        out_shape=(
            jax.ShapeDtypeStruct((rows, cols, width), bf16),
            jax.ShapeDtypeStruct((NQ, width), f32),
            jax.ShapeDtypeStruct((1,), f32),
        ),
        in_specs=[vmem, vmem, vmem, vmem, vmem, hbm, vmem, hbm, vmem, vmem, hbm, hbm, vmem, vmem, smem, vmem],
        out_specs=(vmem, vmem, smem),
        scratch_shapes=[
            pltpu.VMEM((width, hid), bf16),
            pltpu.VMEM((hid, width), bf16),
            pltpu.VMEM((width, width), bf16),
            pltpu.VMEM((width, width), bf16),
            pltpu.VMEM((chunks, rows + 6, cols + 16, LANES), f32),
            pltpu.VMEM((chunks, rows, 16, LANES), f32),
            pltpu.VMEM((chunks, rows, 16, LANES), f32),
            pltpu.VMEM((chunks, rows, cols, LANES), f32),
            pltpu.VMEM((NH * NQ, width), bf16),
            pltpu.VMEM((rows * 8, width), bf16),
            pltpu.VMEM((rows * 8, width), bf16),
            pltpu.VMEM((2, 3, cols, width), bf16),
            pltpu.VMEM((2, rows * 8, width), bf16),
            pltpu.VMEM((4, 32, width), bf16),
            pltpu.VMEM((NQ, wide), f32),
            pltpu.VMEM((GROUP, QROWS, wide), f32),
            pltpu.VMEM((n_far, QROWS, wide), f32),
            pltpu.VMEM((QROWS, wide), f32),
            pltpu.VMEM((GROUP, QROWS, width), f32),
            dma((4,)),
            dma((8,)),
            dma((8,)),
            dma((GROUP,)),
            dma((GROUP,)),
            dma((n_far,)),
            dma((n_far,)),
            dma((GROUP,)),
            dma((GROUP,)),
        ],
        compiler_params=pltpu.CompilerParams(
            collective_id=0, has_side_effects=True, vmem_limit_bytes=40 * 1024 * 1024
        ),
    )(
        features, depth_weight, depth_bias.reshape(1, width), norm_gain.reshape(1, width),
        norm_bias.reshape(1, width), expand_weight, expand_bias.reshape(1, hid), shrink_weight,
        shrink_bias.reshape(1, width), layer_scale.reshape(1, width), key_weight, value_weight,
        queries, class_weight, tissue, slide_label.reshape(1, -1),
    )
    return block, pooled, loss


def solution(mesh):
    everywhere = P()
    cells = P("row", "col", None)
    placed = (cells,) + (everywhere,) * 13 + (P("row", "col"), everywhere)
    return jax.shard_map(
        functools.partial(per_device, mesh.shape["row"], mesh.shape["col"]),
        mesh=mesh,
        in_specs=placed,
        out_specs=(cells, everywhere, everywhere),
        check_vma=False,
    )
```

```python
import functools

import jax
import jax.numpy as jnp
from jax import lax
from jax.experimental import pallas as pl
from jax.experimental.pallas import tpu as pltpu
from jax.sharding import PartitionSpec as P

NH = 8
NQ = 64
TILE = 8
LANES = 128
GROUP_ROWS, GROUP_COLS = 4, 2
GROUP = GROUP_ROWS * GROUP_COLS
QROWS = NQ // GROUP
ORDER = (4, 5, 6, 7, 1, 2, 3, 0)
CALLS = 2
MESH = pl.DeviceIdType.MESH
SIDES = [(-1, 0), (1, 0), (0, -1), (0, 1), (-1, -1), (-1, 1), (1, -1), (1, 1)]


def lane_ids(rows, width):
    return lax.broadcasted_iota(jnp.int32, (rows, width), 1)


def spread(cols, first, width):
    rows = cols.shape[0]
    head = lane_ids(rows, width) // (width // NH)
    out = jnp.zeros((rows, width), jnp.float32)
    for h in range(NH):
        out = jnp.where(head == h, cols[:, first + h : first + h + 1], out)
    return out


def combine(ref, count, width):
    tails = [ref[s, :, width:] for s in range(count)]
    peak = functools.reduce(jnp.maximum, tails)
    weighted = jnp.zeros((QROWS, width), jnp.float32)
    total = jnp.zeros((QROWS, LANES), jnp.float32)
    for s in range(count):
        factor = jnp.exp(tails[s] - peak)
        total = total + pltpu.roll(factor, NH, 1) * tails[s]
        weighted = weighted + ref[s, :, :width] * spread(factor, 0, width)
    return weighted, jnp.where(lane_ids(QROWS, LANES) < NH, peak, total)


def kernel(
    n_row, n_col,
    feat_hbm, dw_hbm, db_hbm, gain_hbm, nbias_hbm, w1_hbm, b1_hbm, w2_hbm, b2_hbm, scale_hbm,
    wk_hbm, wv_hbm, queries_hbm, cw_hbm, tissue_hbm, label_hbm,
    block_ref, pooled_ref, loss_ref,
    feat, dw, db, gain, nbias, w1, b1, w2, b2, scale, wkv, queries, cw, tissue, label, q32, pad, left_pad, right_pad, conv, qbig,
    stage_l, stage_r, halo_rows, halo_cols, halo_corners, msg, got_a, got_b, mine, pooled,
    w_sem, hs_sem, hr_sem, as_sem, ar_sem, bs_sem, br_sem, cs_sem, cr_sem,
):
    rows, cols, width = feat_hbm.shape
    count = rows * cols
    chunks = width // LANES
    row, col = lax.axis_index("row"), lax.axis_index("col")

    sources = (
        (feat_hbm, feat), (dw_hbm, dw), (db_hbm, db), (queries_hbm, queries), (gain_hbm, gain),
        (nbias_hbm, nbias), (w1_hbm, w1), (b1_hbm, b1), (w2_hbm, w2), (b2_hbm, b2),
        (scale_hbm, scale), (wk_hbm, wkv.at[:, pl.ds(0, width)]),
        (wv_hbm, wkv.at[:, pl.ds(width, width)]), (cw_hbm, cw), (tissue_hbm, tissue),
        (label_hbm, label),
    )
    loads = [pltpu.make_async_copy(src, dst, w_sem.at[i]) for i, (src, dst) in enumerate(sources)]
    for load in loads:
        load.start()

    base_row, base_col = (row // GROUP_ROWS) * GROUP_ROWS, (col // GROUP_COLS) * GROUP_COLS
    place = (row - base_row) * GROUP_COLS + (col - base_col)
    over = n_col // GROUP_COLS
    n_far = (n_row // GROUP_ROWS) * over
    far = (row // GROUP_ROWS) * over + col // GROUP_COLS

    def near_peer(step):
        other = (place + step) % GROUP
        return other, (base_row + other // GROUP_COLS, base_col + other % GROUP_COLS)

    def far_peer(step):
        other = (far + step) % n_far
        return other, (
            (other // over) * GROUP_ROWS + place // GROUP_COLS,
            (other % over) * GROUP_COLS + place % GROUP_COLS,
        )

    def present(side):
        dr, dc = side
        ok = None
        for delta, at, size in ((dr, row, n_row), (dc, col, n_col)):
            if delta:
                here = at > 0 if delta < 0 else at < size - 1
                ok = here if ok is None else jnp.logical_and(ok, here)
        return ok

    barrier = pltpu.get_barrier_semaphore()
    for side in SIDES:
        @pl.when(present(side))
        def _(side=side):
            pl.semaphore_signal(
                barrier, inc=1, device_id=(row + side[0], col + side[1]), device_id_type=MESH
            )
    for step in range(1, GROUP):
        pl.semaphore_signal(barrier, inc=1, device_id=near_peer(step)[1], device_id_type=MESH)
    for step in range(1, n_far):
        pl.semaphore_signal(barrier, inc=1, device_id=far_peer(step)[1], device_id_type=MESH)

    loads[0].wait()
    stage_l[...] = feat[:, 0:8, :].astype(jnp.float32).reshape(rows * 8, width).astype(jnp.bfloat16)
    stage_r[...] = (
        feat[:, cols - 8 : cols, :].astype(jnp.float32).reshape(rows * 8, width).astype(jnp.bfloat16)
    )

    landing = {
        (-1, 0): halo_rows.at[0], (1, 0): halo_rows.at[1],
        (0, -1): halo_cols.at[0], (0, 1): halo_cols.at[1],
        (-1, -1): halo_corners.at[0], (-1, 1): halo_corners.at[1],
        (1, -1): halo_corners.at[2], (1, 1): halo_corners.at[3],
    }

    def halo_copy(side):
        dr, dc = side
        if dc == 0:
            src = feat.at[pl.ds(0, 3)] if dr < 0 else feat.at[pl.ds(rows - 3, 3)]
        else:
            src = stage_l if dc < 0 else stage_r
            if dr:
                src = src.at[pl.ds(0 if dr < 0 else rows * 8 - 32, 32)]
        return pltpu.make_async_remote_copy(
            src_ref=src,
            dst_ref=landing[(-dr, -dc)],
            send_sem=hs_sem.at[SIDES.index(side)],
            recv_sem=hr_sem.at[SIDES.index((-dr, -dc))],
            device_id=(row + dr, col + dc),
            device_id_type=MESH,
        )

    greeted = jnp.int32(GROUP - 1 + n_far - 1)
    for side in SIDES:
        greeted = greeted + present(side).astype(jnp.int32)
    pl.semaphore_wait(barrier, greeted)
    for side in SIDES:
        @pl.when(present(side))
        def _(side=side):
            halo_copy(side).start()

        @pl.when(jnp.logical_not(present(side)))
        def _(side=side):
            landing[side][...] = jnp.zeros(landing[side].shape, jnp.bfloat16)

    for c in range(chunks):
        lanes = slice(c * LANES, (c + 1) * LANES)
        pad[c, 3 : 3 + rows, 8 : 8 + cols, :] = feat[:, :, lanes].astype(jnp.float32)
    pad[:, 3 : 3 + rows, 0:8, :] = jnp.zeros((chunks, rows, 8, LANES), jnp.float32)
    pad[:, 3 : 3 + rows, 8 + cols :, :] = jnp.zeros((chunks, rows, 8, LANES), jnp.float32)

    loads[1].wait()
    loads[2].wait()

    def own_part(c, carry):
        at = pl.ds(pl.multiple_of(c * LANES, LANES), LANES)
        acc = [jnp.broadcast_to(db[at].reshape(1, LANES), (cols, LANES)) for _ in range(rows)]
        for b in range(7):
            taps = [dw[a, b : b + 1, at] for a in range(7)]
            for r in range(3, 3 + rows):
                window = pad[c, r, b + 5 : b + 5 + cols, :]
                for a in range(7):
                    if 0 <= r - a < rows:
                        acc[r - a] = acc[r - a] + window * taps[a]
        for i in range(rows):
            conv[c, i] = acc[i]
        return carry

    lax.fori_loop(0, chunks, own_part, 0)

    loads[3].wait()
    q32[...] = queries[...].astype(jnp.float32)
    head = lane_ids(QROWS, width) // (width // NH)
    for at, step in enumerate(ORDER):
        other = near_peer(step)[0] if step else place
        some = q32[pl.ds(pl.multiple_of(other * QROWS, QROWS), QROWS), :]
        heads = [jnp.where(head == h, some, 0.0) for h in range(NH)]
        qbig[at * NH * QROWS : (at + 1) * NH * QROWS, :] = jnp.concatenate(heads, axis=0).astype(jnp.bfloat16)

    for side in SIDES:
        @pl.when(present(side))
        def _(side=side):
            pltpu.make_async_remote_copy(
                src_ref=landing[side],
                dst_ref=landing[side],
                send_sem=hs_sem.at[SIDES.index(side)],
                recv_sem=hr_sem.at[SIDES.index(side)],
                device_id=(row + side[0], col + side[1]),
                device_id_type=MESH,
            ).wait_recv()

    for c in range(chunks):
        lanes = slice(c * LANES, (c + 1) * LANES)
        for end, first in ((0, 0), (1, 3 + rows)):
            pad[c, first : first + 3, 8 : 8 + cols, :] = halo_rows[end, :, :, lanes].astype(jnp.float32)
            for side in range(2):
                corner = halo_corners[end * 2 + side, :, lanes].astype(jnp.float32).reshape(4, 8, LANES)
                start = 0 if side == 0 else 8 + cols
                pad[c, first : first + 3, start : start + 8, :] = corner[1:4] if end == 0 else corner[0:3]
        left_pad[c, :, 0:8, :] = halo_cols[0, :, lanes].astype(jnp.float32).reshape(rows, 8, LANES)
        right_pad[c, :, 8:16, :] = halo_cols[1, :, lanes].astype(jnp.float32).reshape(rows, 8, LANES)
    left_pad[:, :, 8:16, :] = jnp.zeros((chunks, rows, 8, LANES), jnp.float32)
    right_pad[:, :, 0:8, :] = jnp.zeros((chunks, rows, 8, LANES), jnp.float32)

    def border_part(c, carry):
        at = pl.ds(pl.multiple_of(c * LANES, LANES), LANES)
        acc = [conv[c, i] for i in range(rows)]
        low = [jnp.zeros((8, LANES), jnp.float32) for _ in range(rows)]
        high = [jnp.zeros((8, LANES), jnp.float32) for _ in range(rows)]
        for b in range(7):
            taps = [dw[a, b : b + 1, at] for a in range(7)]
            for r in list(range(3)) + list(range(3 + rows, 6 + rows)):
                window = pad[c, r, b + 5 : b + 5 + cols, :]
                for a in range(7):
                    if 0 <= r - a < rows:
                        acc[r - a] = acc[r - a] + window * taps[a]
            if b != 3:
                side, edge, start = (low, left_pad, b + 5) if b < 3 else (high, right_pad, b - 3)
                for r in range(3, 3 + rows):
                    window = edge[c, r - 3, start : start + 8, :]
                    for a in range(7):
                        if 0 <= r - a < rows:
                            side[r - a] = side[r - a] + window * taps[a]
        for i in range(rows):
            conv[c, i] = acc[i]
            conv[c, i, 0:8, :] = conv[c, i, 0:8, :] + low[i]
            conv[c, i, cols - 8 : cols, :] = conv[c, i, cols - 8 : cols, :] + high[i]
        return carry

    lax.fori_loop(0, chunks, border_part, 0)

    full = jnp.concatenate([conv[c].reshape(count, LANES) for c in range(chunks)], axis=1)
    center = jnp.mean(full, axis=-1, keepdims=True)
    off = full - center
    variance = jnp.mean(off * off, axis=-1, keepdims=True)
    for load in loads[4:11]:
        load.wait()
    normed = (
        off * lax.rsqrt(variance + 1e-06) * gain[...].reshape(1, width) + nbias[...].reshape(1, width)
    ).astype(jnp.bfloat16)

    hid = w1.shape[1]
    piece = 384
    shrunk = jnp.zeros((count, width), jnp.float32)
    for start in range(0, hid, piece):
        part = slice(start, start + piece)
        expanded = jnp.dot(normed, w1[:, part], preferred_element_type=jnp.float32) + b1[part].reshape(1, piece)
        hidden = (0.5 * expanded * (1.0 + lax.erf(expanded * 0.5**0.5))).astype(jnp.bfloat16)
        shrunk = shrunk + jnp.dot(hidden, w2[part, :], preferred_element_type=jnp.float32)
    shrunk = shrunk + b2[...].reshape(1, width)
    inputs = feat[...].astype(jnp.float32).reshape(count, width)
    block = (inputs + scale[...].reshape(1, width) * shrunk).astype(jnp.bfloat16)
    block_ref[...] = block.reshape(rows, cols, width)

    for load in loads[11:]:
        load.wait()
    both = jnp.dot(block, wkv[...], preferred_element_type=jnp.float32).astype(jnp.bfloat16)
    keys, values = both[:, :width], both[:, width:]
    cell = lane_ids(1, count)
    tile = (cell // cols) // TILE * (cols // TILE) + (cell % cols) // TILE
    alive = jnp.zeros((1, count), jnp.int32)
    for i in range(rows // TILE):
        for j in range(cols // TILE):
            alive = jnp.where(tile == i * (cols // TILE) + j, tissue[i, j], alive)
    live = alive > 0
    lane = lane_ids(QROWS, LANES)
    copies_a = []
    per_call = GROUP // CALLS
    size = NH * QROWS
    for call in range(CALLS):
        scores = lax.dot_general(
            qbig[call * per_call * size : (call + 1) * per_call * size, :], keys,
            (((1,), (1,)), ((), ())), preferred_element_type=jnp.float32,
        ) * (width // NH) ** (-0.5)
        scores = jnp.where(live, scores, -1e30)
        peak = jnp.max(scores, axis=1, keepdims=True)
        weights = jnp.where(live, jnp.exp(scores - peak), 0.0)
        total = jnp.sum(weights, axis=1, keepdims=True)
        mixed = jnp.dot(weights.astype(jnp.bfloat16), values, preferred_element_type=jnp.float32)
        for i in range(per_call):
            at = call * per_call + i
            weighted = jnp.zeros((QROWS, width), jnp.float32)
            tail = jnp.zeros((QROWS, LANES), jnp.float32)
            for h in range(NH):
                own = slice(i * size + h * QROWS, i * size + (h + 1) * QROWS)
                weighted = jnp.where(head == h, mixed[own], weighted)
                tail = jnp.where(lane == h, peak[own], tail)
                tail = jnp.where(lane == NH + h, total[own], tail)
            step = ORDER[at]
            if step == 0:
                got_a[place, :, :width] = weighted
                got_a[place, :, width:] = tail
                continue
            msg[at, :, :width] = weighted
            msg[at, :, width:] = tail
            copies_a.append(pltpu.make_async_remote_copy(
                src_ref=msg.at[at],
                dst_ref=got_a.at[place],
                send_sem=as_sem.at[step],
                recv_sem=ar_sem.at[place],
                device_id=near_peer(step)[1],
                device_id_type=MESH,
            ))
            copies_a[-1].start()

    def arrival(dst, sem):
        return pltpu.make_async_remote_copy(
            src_ref=dst, dst_ref=dst, send_sem=as_sem.at[0], recv_sem=sem,
            device_id=near_peer(1)[1], device_id_type=MESH,
        )

    for step in range(1, GROUP):
        other = near_peer(step)[0]
        arrival(got_a.at[other], ar_sem.at[other]).wait_recv()
    weighted, tail = combine(got_a, GROUP, width)

    if n_far > 1:
        mine[:, :width] = weighted
        mine[:, width:] = tail
        copies_b = []
        for step in range(1, n_far):
            other, device = far_peer(step)
            copies_b.append(pltpu.make_async_remote_copy(
                src_ref=mine,
                dst_ref=got_b.at[far],
                send_sem=bs_sem.at[step],
                recv_sem=br_sem.at[far],
                device_id=device,
                device_id_type=MESH,
            ))
            copies_b[-1].start()
        got_b[far] = mine[...]
        for step in range(1, n_far):
            other = far_peer(step)[0]
            arrival(got_b.at[other], br_sem.at[other]).wait_recv()
        weighted, tail = combine(got_b, n_far, width)
    pooled[place] = weighted / spread(tail, NH, width)

    copies_c = []
    for step in range(1, GROUP):
        other, device = near_peer(step)
        copies_c.append(pltpu.make_async_remote_copy(
            src_ref=pooled.at[place],
            dst_ref=pooled.at[place],
            send_sem=cs_sem.at[step],
            recv_sem=cr_sem.at[place],
            device_id=device,
            device_id_type=MESH,
        ))
        copies_c[-1].start()
    for step in range(1, GROUP):
        other = near_peer(step)[0]
        arrival(pooled.at[other], cr_sem.at[other]).wait_recv()
    result = pooled[...].reshape(NQ, width)
    pooled_ref[...] = result
    summed = jnp.sum(result, axis=0, keepdims=True)
    logits = jnp.sum(summed * cw[...], axis=1, keepdims=True)
    soft = jnp.maximum(logits, 0.0) + jnp.log1p(jnp.exp(-jnp.abs(logits)))
    n_lab = cw.shape[0]
    which = lax.broadcasted_iota(jnp.int32, (n_lab, 1), 0)
    truth = jnp.zeros((n_lab, 1), jnp.int32)
    for k in range(n_lab):
        truth = jnp.where(which == k, label[k], truth)
    loss_ref[0] = jnp.sum(soft - truth.astype(jnp.float32) * logits)

    for side in SIDES:
        @pl.when(present(side))
        def _(side=side):
            halo_copy(side).wait_send()
    for copy in copies_a:
        copy.wait_send()
    if n_far > 1:
        for copy in copies_b:
            copy.wait_send()
    for copy in copies_c:
        copy.wait_send()


def per_device(
    n_row, n_col,
    features, depth_weight, depth_bias, norm_gain, norm_bias, expand_weight, expand_bias,
    shrink_weight, shrink_bias, layer_scale, key_weight, value_weight, queries, class_weight,
    tissue, slide_label,
):
    rows, cols, width = features.shape
    hid = expand_weight.shape[1]
    chunks = width // LANES
    n_far = (n_row // GROUP_ROWS) * (n_col // GROUP_COLS)
    vmem = pl.BlockSpec(memory_space=pltpu.VMEM)
    smem = pl.BlockSpec(memory_space=pltpu.SMEM)
    hbm = pl.BlockSpec(memory_space=pltpu.HBM)
    wide = width + LANES
    f32, bf16 = jnp.float32, jnp.bfloat16
    dma = pltpu.SemaphoreType.DMA
    block, pooled, loss = pl.pallas_call(
        functools.partial(kernel, n_row, n_col),
        out_shape=(
            jax.ShapeDtypeStruct((rows, cols, width), bf16),
            jax.ShapeDtypeStruct((NQ, width), f32),
            jax.ShapeDtypeStruct((1,), f32),
        ),
        in_specs=[hbm] * 16,
        out_specs=(vmem, vmem, smem),
        scratch_shapes=[
            pltpu.VMEM((rows, cols, width), bf16),
            pltpu.VMEM(depth_weight.shape, f32),
            pltpu.VMEM((width,), f32),
            pltpu.VMEM((width,), f32),
            pltpu.VMEM((width,), f32),
            pltpu.VMEM((width, hid), bf16),
            pltpu.VMEM((hid,), f32),
            pltpu.VMEM((hid, width), bf16),
            pltpu.VMEM((width,), f32),
            pltpu.VMEM((width,), f32),
            pltpu.VMEM((width, 2 * width), bf16),
            pltpu.VMEM((NQ, width), bf16),
            pltpu.VMEM((class_weight.shape[1], width), f32),
            pltpu.SMEM(tissue.shape, jnp.int32),
            pltpu.SMEM(slide_label.shape, jnp.int32),
            pltpu.VMEM((NQ, width), f32),
            pltpu.VMEM((chunks, rows + 6, cols + 16, LANES), f32),
            pltpu.VMEM((chunks, rows, 16, LANES), f32),
            pltpu.VMEM((chunks, rows, 16, LANES), f32),
            pltpu.VMEM((chunks, rows, cols, LANES), f32),
            pltpu.VMEM((NH * NQ, width), bf16),
            pltpu.VMEM((rows * 8, width), bf16),
            pltpu.VMEM((rows * 8, width), bf16),
            pltpu.VMEM((2, 3, cols, width), bf16),
            pltpu.VMEM((2, rows * 8, width), bf16),
            pltpu.VMEM((4, 32, width), bf16),
            pltpu.VMEM((GROUP, QROWS, wide), f32),
            pltpu.VMEM((GROUP, QROWS, wide), f32),
            pltpu.VMEM((n_far, QROWS, wide), f32),
            pltpu.VMEM((QROWS, wide), f32),
            pltpu.VMEM((GROUP, QROWS, width), f32),
            dma((16,)),
            dma((8,)),
            dma((8,)),
            dma((GROUP,)),
            dma((GROUP,)),
            dma((n_far,)),
            dma((n_far,)),
            dma((GROUP,)),
            dma((GROUP,)),
        ],
        compiler_params=pltpu.CompilerParams(
            collective_id=0, has_side_effects=True, vmem_limit_bytes=63 * 1024 * 1024
        ),
    )(
        features, depth_weight, depth_bias, norm_gain, norm_bias, expand_weight, expand_bias,
        shrink_weight, shrink_bias, layer_scale, key_weight, value_weight, queries, class_weight.T,
        tissue, slide_label,
    )
    return block, pooled, loss


def solution(mesh):
    everywhere = P()
    cells = P("row", "col", None)
    placed = (cells,) + (everywhere,) * 13 + (P("row", "col"), everywhere)
    return jax.shard_map(
        functools.partial(per_device, mesh.shape["row"], mesh.shape["col"]),
        mesh=mesh,
        in_specs=placed,
        out_specs=(cells, everywhere, everywhere),
        check_vma=False,
    )
```

```python
import functools

import jax
import jax.numpy as jnp
from jax import lax
from jax.experimental import pallas as pl
from jax.experimental.pallas import tpu as pltpu
from jax.sharding import PartitionSpec as P

NH = 8
NQ = 64
TILE = 8
LANES = 128
GROUP_ROWS, GROUP_COLS = 4, 2
GROUP = GROUP_ROWS * GROUP_COLS
QROWS = NQ // GROUP
ORDER = (4, 5, 6, 7, 1, 2, 3, 0)
CALLS = 2
MESH = pl.DeviceIdType.MESH
SIDES = [(-1, 0), (1, 0), (0, -1), (0, 1), (-1, -1), (-1, 1), (1, -1), (1, 1)]


def lane_ids(rows, width):
    return lax.broadcasted_iota(jnp.int32, (rows, width), 1)


def spread(cols, first, width):
    rows = cols.shape[0]
    head = lane_ids(rows, width) // (width // NH)
    out = jnp.zeros((rows, width), jnp.float32)
    for h in range(NH):
        out = jnp.where(head == h, cols[:, first + h : first + h + 1], out)
    return out


def combine(ref, count, width):
    tails = [ref[s, :, width:] for s in range(count)]
    peak = functools.reduce(jnp.maximum, tails)
    weighted = jnp.zeros((QROWS, width), jnp.float32)
    total = jnp.zeros((QROWS, LANES), jnp.float32)
    for s in range(count):
        factor = jnp.exp(tails[s] - peak)
        total = total + pltpu.roll(factor, NH, 1) * tails[s]
        weighted = weighted + ref[s, :, :width] * spread(factor, 0, width)
    return weighted, jnp.where(lane_ids(QROWS, LANES) < NH, peak, total)


def kernel(
    n_row, n_col,
    feat_hbm, dw_hbm, db_hbm, gain_hbm, nbias_hbm, w1_hbm, b1_hbm, w2_hbm, b2_hbm, scale_hbm,
    wk_hbm, wv_hbm, queries_hbm, cw_hbm, tissue_hbm, label_hbm,
    block_ref, pooled_ref, loss_ref,
    feat, dw, db, gain, nbias, w1, b1, w2, b2, scale, wkv, queries, cw, tissue, label, q32, pad, left_pad, right_pad, conv, qbig,
    stage_l, stage_r, halo_rows, halo_cols, halo_corners, msg, got_a, got_b, mine, pooled,
    w_sem, hs_sem, hr_sem, as_sem, ar_sem, bs_sem, br_sem, cs_sem, cr_sem,
):
    rows, cols, width = feat_hbm.shape
    count = rows * cols
    chunks = width // LANES
    row, col = lax.axis_index("row"), lax.axis_index("col")

    sources = (
        (feat_hbm, feat), (dw_hbm, dw), (db_hbm, db), (queries_hbm, queries), (gain_hbm, gain),
        (nbias_hbm, nbias), (w1_hbm, w1), (b1_hbm, b1), (w2_hbm, w2), (b2_hbm, b2),
        (scale_hbm, scale), (wk_hbm, wkv.at[:, pl.ds(0, width)]),
        (wv_hbm, wkv.at[:, pl.ds(width, width)]), (cw_hbm, cw), (tissue_hbm, tissue),
        (label_hbm, label),
    )
    loads = [pltpu.make_async_copy(src, dst, w_sem.at[i]) for i, (src, dst) in enumerate(sources)]
    for load in loads:
        load.start()

    base_row, base_col = (row // GROUP_ROWS) * GROUP_ROWS, (col // GROUP_COLS) * GROUP_COLS
    place = (row - base_row) * GROUP_COLS + (col - base_col)
    over = n_col // GROUP_COLS
    n_far = (n_row // GROUP_ROWS) * over
    far = (row // GROUP_ROWS) * over + col // GROUP_COLS

    def near_peer(step):
        other = (place + step) % GROUP
        return other, (base_row + other // GROUP_COLS, base_col + other % GROUP_COLS)

    def far_peer(step):
        other = (far + step) % n_far
        return other, (
            (other // over) * GROUP_ROWS + place // GROUP_COLS,
            (other % over) * GROUP_COLS + place % GROUP_COLS,
        )

    def present(side):
        dr, dc = side
        ok = None
        for delta, at, size in ((dr, row, n_row), (dc, col, n_col)):
            if delta:
                here = at > 0 if delta < 0 else at < size - 1
                ok = here if ok is None else jnp.logical_and(ok, here)
        return ok

    barrier = pltpu.get_barrier_semaphore()
    for side in SIDES:
        @pl.when(present(side))
        def _(side=side):
            pl.semaphore_signal(
                barrier, inc=1, device_id=(row + side[0], col + side[1]), device_id_type=MESH
            )
    for step in range(1, GROUP):
        pl.semaphore_signal(barrier, inc=1, device_id=near_peer(step)[1], device_id_type=MESH)
    for step in range(1, n_far):
        pl.semaphore_signal(barrier, inc=1, device_id=far_peer(step)[1], device_id_type=MESH)

    loads[0].wait()
    stage_l[...] = feat[:, 0:8, :].astype(jnp.float32).reshape(rows * 8, width).astype(jnp.bfloat16)
    stage_r[...] = (
        feat[:, cols - 8 : cols, :].astype(jnp.float32).reshape(rows * 8, width).astype(jnp.bfloat16)
    )

    landing = {
        (-1, 0): halo_rows.at[0], (1, 0): halo_rows.at[1],
        (0, -1): halo_cols.at[0], (0, 1): halo_cols.at[1],
        (-1, -1): halo_corners.at[0], (-1, 1): halo_corners.at[1],
        (1, -1): halo_corners.at[2], (1, 1): halo_corners.at[3],
    }

    def halo_copy(side):
        dr, dc = side
        if dc == 0:
            src = feat.at[pl.ds(0, 3)] if dr < 0 else feat.at[pl.ds(rows - 3, 3)]
        else:
            src = stage_l if dc < 0 else stage_r
            if dr:
                src = src.at[pl.ds(0 if dr < 0 else rows * 8 - 32, 32)]
        return pltpu.make_async_remote_copy(
            src_ref=src,
            dst_ref=landing[(-dr, -dc)],
            send_sem=hs_sem.at[SIDES.index(side)],
            recv_sem=hr_sem.at[SIDES.index((-dr, -dc))],
            device_id=(row + dr, col + dc),
            device_id_type=MESH,
        )

    greeted = jnp.int32(GROUP - 1 + n_far - 1)
    for side in SIDES:
        greeted = greeted + present(side).astype(jnp.int32)
    pl.semaphore_wait(barrier, greeted)
    for side in SIDES:
        @pl.when(present(side))
        def _(side=side):
            halo_copy(side).start()

        @pl.when(jnp.logical_not(present(side)))
        def _(side=side):
            landing[side][...] = jnp.zeros(landing[side].shape, jnp.bfloat16)

    for c in range(chunks):
        lanes = slice(c * LANES, (c + 1) * LANES)
        pad[c, 3 : 3 + rows, 8 : 8 + cols, :] = feat[:, :, lanes].astype(jnp.float32)
    pad[:, 3 : 3 + rows, 0:8, :] = jnp.zeros((chunks, rows, 8, LANES), jnp.float32)
    pad[:, 3 : 3 + rows, 8 + cols :, :] = jnp.zeros((chunks, rows, 8, LANES), jnp.float32)

    loads[1].wait()
    loads[2].wait()

    def own_part(c, carry):
        at = pl.ds(pl.multiple_of(c * LANES, LANES), LANES)
        acc = [jnp.broadcast_to(db[at].reshape(1, LANES), (cols, LANES)) for _ in range(rows)]
        for b in range(7):
            taps = [dw[a, b : b + 1, at] for a in range(7)]
            for r in range(3, 3 + rows):
                window = pad[c, r, b + 5 : b + 5 + cols, :]
                for a in range(7):
                    if 0 <= r - a < rows:
                        acc[r - a] = acc[r - a] + window * taps[a]
        for i in range(rows):
            conv[c, i] = acc[i]
        return carry

    lax.fori_loop(0, chunks, own_part, 0)

    loads[3].wait()
    q32[...] = queries[...].astype(jnp.float32)
    head = lane_ids(QROWS, width) // (width // NH)
    for at, step in enumerate(ORDER):
        other = near_peer(step)[0] if step else place
        some = q32[pl.ds(pl.multiple_of(other * QROWS, QROWS), QROWS), :]
        heads = [jnp.where(head == h, some, 0.0) for h in range(NH)]
        qbig[at * NH * QROWS : (at + 1) * NH * QROWS, :] = jnp.concatenate(heads, axis=0).astype(jnp.bfloat16)

    for side in SIDES:
        @pl.when(present(side))
        def _(side=side):
            pltpu.make_async_remote_copy(
                src_ref=landing[side],
                dst_ref=landing[side],
                send_sem=hs_sem.at[SIDES.index(side)],
                recv_sem=hr_sem.at[SIDES.index(side)],
                device_id=(row + side[0], col + side[1]),
                device_id_type=MESH,
            ).wait_recv()

    for c in range(chunks):
        lanes = slice(c * LANES, (c + 1) * LANES)
        for end, first in ((0, 0), (1, 3 + rows)):
            pad[c, first : first + 3, 8 : 8 + cols, :] = halo_rows[end, :, :, lanes].astype(jnp.float32)
            for side in range(2):
                corner = halo_corners[end * 2 + side, :, lanes].astype(jnp.float32).reshape(4, 8, LANES)
                start = 0 if side == 0 else 8 + cols
                pad[c, first : first + 3, start : start + 8, :] = corner[1:4] if end == 0 else corner[0:3]
        left_pad[c, :, 0:8, :] = halo_cols[0, :, lanes].astype(jnp.float32).reshape(rows, 8, LANES)
        right_pad[c, :, 8:16, :] = halo_cols[1, :, lanes].astype(jnp.float32).reshape(rows, 8, LANES)
    left_pad[:, :, 8:16, :] = jnp.zeros((chunks, rows, 8, LANES), jnp.float32)
    right_pad[:, :, 0:8, :] = jnp.zeros((chunks, rows, 8, LANES), jnp.float32)

    def border_part(c, carry):
        at = pl.ds(pl.multiple_of(c * LANES, LANES), LANES)
        acc = [conv[c, i] for i in range(rows)]
        low = [jnp.zeros((8, LANES), jnp.float32) for _ in range(rows)]
        high = [jnp.zeros((8, LANES), jnp.float32) for _ in range(rows)]
        for b in range(7):
            taps = [dw[a, b : b + 1, at] for a in range(7)]
            for r in list(range(3)) + list(range(3 + rows, 6 + rows)):
                window = pad[c, r, b + 5 : b + 5 + cols, :]
                for a in range(7):
                    if 0 <= r - a < rows:
                        acc[r - a] = acc[r - a] + window * taps[a]
            if b != 3:
                side, edge, start = (low, left_pad, b + 5) if b < 3 else (high, right_pad, b - 3)
                for r in range(3, 3 + rows):
                    window = edge[c, r - 3, start : start + 8, :]
                    for a in range(7):
                        if 0 <= r - a < rows:
                            side[r - a] = side[r - a] + window * taps[a]
        for i in range(rows):
            conv[c, i] = acc[i]
            conv[c, i, 0:8, :] = conv[c, i, 0:8, :] + low[i]
            conv[c, i, cols - 8 : cols, :] = conv[c, i, cols - 8 : cols, :] + high[i]
        return carry

    lax.fori_loop(0, chunks, border_part, 0)

    full = jnp.concatenate([conv[c].reshape(count, LANES) for c in range(chunks)], axis=1)
    center = jnp.mean(full, axis=-1, keepdims=True)
    off = full - center
    variance = jnp.mean(off * off, axis=-1, keepdims=True)
    for load in loads[4:11]:
        load.wait()
    normed = (
        off * lax.rsqrt(variance + 1e-06) * gain[...].reshape(1, width) + nbias[...].reshape(1, width)
    ).astype(jnp.bfloat16)

    hid = w1.shape[1]
    piece = 256
    shrunk = jnp.zeros((count, width), jnp.float32)
    starts = list(range(0, hid, piece))

    def expand(start):
        part = slice(start, start + piece)
        wide = jnp.dot(normed, w1[:, part], preferred_element_type=jnp.float32)
        return wide + b1[part].reshape(1, piece)

    expanded = expand(starts[0])
    for i, start in enumerate(starts):
        following = expand(starts[i + 1]) if i + 1 < len(starts) else None
        hidden = (0.5 * expanded * (1.0 + lax.erf(expanded * 0.5**0.5))).astype(jnp.bfloat16)
        shrunk = shrunk + jnp.dot(
            hidden, w2[start : start + piece, :], preferred_element_type=jnp.float32
        )
        expanded = following
    shrunk = shrunk + b2[...].reshape(1, width)
    inputs = feat[...].astype(jnp.float32).reshape(count, width)
    block = (inputs + scale[...].reshape(1, width) * shrunk).astype(jnp.bfloat16)
    block_ref[...] = block.reshape(rows, cols, width)

    for load in loads[11:]:
        load.wait()
    both = jnp.dot(block, wkv[...], preferred_element_type=jnp.float32).astype(jnp.bfloat16)
    keys, values = both[:, :width], both[:, width:]
    cell = lane_ids(1, count)
    tile = (cell // cols) // TILE * (cols // TILE) + (cell % cols) // TILE
    alive = jnp.zeros((1, count), jnp.int32)
    for i in range(rows // TILE):
        for j in range(cols // TILE):
            alive = jnp.where(tile == i * (cols // TILE) + j, tissue[i, j], alive)
    live = alive > 0
    lane = lane_ids(QROWS, LANES)
    copies_a = []
    per_call = GROUP // CALLS
    size = NH * QROWS
    for call in range(CALLS):
        scores = lax.dot_general(
            qbig[call * per_call * size : (call + 1) * per_call * size, :], keys,
            (((1,), (1,)), ((), ())), preferred_element_type=jnp.float32,
        ) * (width // NH) ** (-0.5)
        scores = jnp.where(live, scores, -1e30)
        peak = jnp.max(scores, axis=1, keepdims=True)
        weights = jnp.where(live, jnp.exp(scores - peak), 0.0)
        total = jnp.sum(weights, axis=1, keepdims=True)
        mixed = jnp.dot(weights.astype(jnp.bfloat16), values, preferred_element_type=jnp.float32)
        for i in range(per_call):
            at = call * per_call + i
            weighted = jnp.zeros((QROWS, width), jnp.float32)
            tail = jnp.zeros((QROWS, LANES), jnp.float32)
            for h in range(NH):
                own = slice(i * size + h * QROWS, i * size + (h + 1) * QROWS)
                weighted = jnp.where(head == h, mixed[own], weighted)
                tail = jnp.where(lane == h, peak[own], tail)
                tail = jnp.where(lane == NH + h, total[own], tail)
            step = ORDER[at]
            if step == 0:
                got_a[place, :, :width] = weighted
                got_a[place, :, width:] = tail
                continue
            msg[at, :, :width] = weighted
            msg[at, :, width:] = tail
            copies_a.append(pltpu.make_async_remote_copy(
                src_ref=msg.at[at],
                dst_ref=got_a.at[place],
                send_sem=as_sem.at[step],
                recv_sem=ar_sem.at[place],
                device_id=near_peer(step)[1],
                device_id_type=MESH,
            ))
            copies_a[-1].start()

    def arrival(dst, sem):
        return pltpu.make_async_remote_copy(
            src_ref=dst, dst_ref=dst, send_sem=as_sem.at[0], recv_sem=sem,
            device_id=near_peer(1)[1], device_id_type=MESH,
        )

    for step in range(1, GROUP):
        other = near_peer(step)[0]
        arrival(got_a.at[other], ar_sem.at[other]).wait_recv()
    weighted, tail = combine(got_a, GROUP, width)

    if n_far > 1:
        mine[:, :width] = weighted
        mine[:, width:] = tail
        copies_b = []
        for step in range(1, n_far):
            other, device = far_peer(step)
            copies_b.append(pltpu.make_async_remote_copy(
                src_ref=mine,
                dst_ref=got_b.at[far],
                send_sem=bs_sem.at[step],
                recv_sem=br_sem.at[far],
                device_id=device,
                device_id_type=MESH,
            ))
            copies_b[-1].start()
        got_b[far] = mine[...]
        for step in range(1, n_far):
            other = far_peer(step)[0]
            arrival(got_b.at[other], br_sem.at[other]).wait_recv()
        weighted, tail = combine(got_b, n_far, width)
    pooled[place] = weighted / spread(tail, NH, width)

    copies_c = []
    for step in range(1, GROUP):
        other, device = near_peer(step)
        copies_c.append(pltpu.make_async_remote_copy(
            src_ref=pooled.at[place],
            dst_ref=pooled.at[place],
            send_sem=cs_sem.at[step],
            recv_sem=cr_sem.at[place],
            device_id=device,
            device_id_type=MESH,
        ))
        copies_c[-1].start()
    for step in range(1, GROUP):
        other = near_peer(step)[0]
        arrival(pooled.at[other], cr_sem.at[other]).wait_recv()
    result = pooled[...].reshape(NQ, width)
    pooled_ref[...] = result
    summed = jnp.sum(result, axis=0, keepdims=True)
    logits = jnp.sum(summed * cw[...], axis=1, keepdims=True)
    soft = jnp.maximum(logits, 0.0) + jnp.log1p(jnp.exp(-jnp.abs(logits)))
    n_lab = cw.shape[0]
    which = lax.broadcasted_iota(jnp.int32, (n_lab, 1), 0)
    truth = jnp.zeros((n_lab, 1), jnp.int32)
    for k in range(n_lab):
        truth = jnp.where(which == k, label[k], truth)
    loss_ref[0] = jnp.sum(soft - truth.astype(jnp.float32) * logits)

    for side in SIDES:
        @pl.when(present(side))
        def _(side=side):
            halo_copy(side).wait_send()
    for copy in copies_a:
        copy.wait_send()
    if n_far > 1:
        for copy in copies_b:
            copy.wait_send()
    for copy in copies_c:
        copy.wait_send()


def per_device(
    n_row, n_col,
    features, depth_weight, depth_bias, norm_gain, norm_bias, expand_weight, expand_bias,
    shrink_weight, shrink_bias, layer_scale, key_weight, value_weight, queries, class_weight,
    tissue, slide_label,
):
    rows, cols, width = features.shape
    hid = expand_weight.shape[1]
    chunks = width // LANES
    n_far = (n_row // GROUP_ROWS) * (n_col // GROUP_COLS)
    vmem = pl.BlockSpec(memory_space=pltpu.VMEM)
    smem = pl.BlockSpec(memory_space=pltpu.SMEM)
    hbm = pl.BlockSpec(memory_space=pltpu.HBM)
    wide = width + LANES
    f32, bf16 = jnp.float32, jnp.bfloat16
    dma = pltpu.SemaphoreType.DMA
    block, pooled, loss = pl.pallas_call(
        functools.partial(kernel, n_row, n_col),
        out_shape=(
            pltpu.VMEM((rows, cols, width), bf16),
            pltpu.VMEM((NQ, width), f32),
            jax.ShapeDtypeStruct((1,), f32),
        ),
        in_specs=[hbm] * 16,
        out_specs=(vmem, vmem, smem),
        scratch_shapes=[
            pltpu.VMEM((rows, cols, width), bf16),
            pltpu.VMEM(depth_weight.shape, f32),
            pltpu.VMEM((width,), f32),
            pltpu.VMEM((width,), f32),
            pltpu.VMEM((width,), f32),
            pltpu.VMEM((width, hid), bf16),
            pltpu.VMEM((hid,), f32),
            pltpu.VMEM((hid, width), bf16),
            pltpu.VMEM((width,), f32),
            pltpu.VMEM((width,), f32),
            pltpu.VMEM((width, 2 * width), bf16),
            pltpu.VMEM((NQ, width), bf16),
            pltpu.VMEM((class_weight.shape[1], width), f32),
            pltpu.SMEM(tissue.shape, jnp.int32),
            pltpu.SMEM(slide_label.shape, jnp.int32),
            pltpu.VMEM((NQ, width), f32),
            pltpu.VMEM((chunks, rows + 6, cols + 16, LANES), f32),
            pltpu.VMEM((chunks, rows, 16, LANES), f32),
            pltpu.VMEM((chunks, rows, 16, LANES), f32),
            pltpu.VMEM((chunks, rows, cols, LANES), f32),
            pltpu.VMEM((NH * NQ, width), bf16),
            pltpu.VMEM((rows * 8, width), bf16),
            pltpu.VMEM((rows * 8, width), bf16),
            pltpu.VMEM((2, 3, cols, width), bf16),
            pltpu.VMEM((2, rows * 8, width), bf16),
            pltpu.VMEM((4, 32, width), bf16),
            pltpu.VMEM((GROUP, QROWS, wide), f32),
            pltpu.VMEM((GROUP, QROWS, wide), f32),
            pltpu.VMEM((n_far, QROWS, wide), f32),
            pltpu.VMEM((QROWS, wide), f32),
            pltpu.VMEM((GROUP, QROWS, width), f32),
            dma((16,)),
            dma((8,)),
            dma((8,)),
            dma((GROUP,)),
            dma((GROUP,)),
            dma((n_far,)),
            dma((n_far,)),
            dma((GROUP,)),
            dma((GROUP,)),
        ],
        compiler_params=pltpu.CompilerParams(
            collective_id=0, has_side_effects=True, vmem_limit_bytes=63 * 1024 * 1024
        ),
    )(
        features, depth_weight, depth_bias, norm_gain, norm_bias, expand_weight, expand_bias,
        shrink_weight, shrink_bias, layer_scale, key_weight, value_weight, queries, class_weight.T,
        tissue, slide_label,
    )
    return block, pooled, loss


def solution(mesh):
    everywhere = P()
    cells = P("row", "col", None)
    placed = (cells,) + (everywhere,) * 13 + (P("row", "col"), everywhere)
    return jax.shard_map(
        functools.partial(per_device, mesh.shape["row"], mesh.shape["col"]),
        mesh=mesh,
        in_specs=placed,
        out_specs=(cells, everywhere, everywhere),
        check_vma=False,
    )
```

```python
import functools

import jax
import jax.numpy as jnp
from jax import lax
from jax.experimental import pallas as pl
from jax.experimental.pallas import tpu as pltpu
from jax.sharding import PartitionSpec as P

NH = 8
NQ = 64
TILE = 8
LANES = 128
GROUP_ROWS, GROUP_COLS = 4, 2
GROUP = GROUP_ROWS * GROUP_COLS
QROWS = NQ // GROUP
ORDER = (4, 5, 6, 7, 1, 2, 3, 0)
CALLS = 2
MESH = pl.DeviceIdType.MESH
SIDES = [(-1, 0), (1, 0), (0, -1), (0, 1), (-1, -1), (-1, 1), (1, -1), (1, 1)]


def lane_ids(rows, width):
    return lax.broadcasted_iota(jnp.int32, (rows, width), 1)


def spread(cols, first, width):
    rows = cols.shape[0]
    head = lane_ids(rows, width) // (width // NH)
    out = jnp.zeros((rows, width), jnp.float32)
    for h in range(NH):
        out = jnp.where(head == h, cols[:, first + h : first + h + 1], out)
    return out


def gelu(x):
    size = jnp.abs(x)
    t = 1.0 / (1.0 + (0.3275911 * 0.5**0.5) * size)
    poly = 0.5 * 1.061405429
    for term in (-1.453152027, 1.421413741, -0.284496736, 0.254829592):
        poly = poly * t + 0.5 * term
    return jnp.maximum(x, 0.0) - size * (poly * t) * jnp.exp(-0.5 * (x * x))


def combine(ref, count, width):
    tails = [ref[s, :, width:] for s in range(count)]
    peak = functools.reduce(jnp.maximum, tails)
    weighted = jnp.zeros((QROWS, width), jnp.float32)
    total = jnp.zeros((QROWS, LANES), jnp.float32)
    for s in range(count):
        factor = jnp.exp(tails[s] - peak)
        total = total + pltpu.roll(factor, NH, 1) * tails[s]
        weighted = weighted + ref[s, :, :width] * spread(factor, 0, width)
    return weighted, jnp.where(lane_ids(QROWS, LANES) < NH, peak, total)


def kernel(
    n_row, n_col,
    feat_hbm, dw_hbm, db_hbm, gain_hbm, nbias_hbm, w1_hbm, b1_hbm, w2_hbm, b2_hbm, scale_hbm,
    wk_hbm, wv_hbm, queries_hbm, cw_hbm, tissue_hbm, label_hbm,
    block_ref, pooled_ref, loss_ref,
    feat, dw, db, gain, nbias, w1, b1, w2, b2, scale, wkv, queries, cw, tissue, label, q32, pad, left_pad, right_pad, conv, qbig,
    stage_l, stage_r, halo_rows, halo_cols, halo_corners, msg, got_a, got_b, mine, pooled,
    w_sem, hs_sem, hr_sem, as_sem, ar_sem, bs_sem, br_sem, cs_sem, cr_sem,
):
    rows, cols, width = feat_hbm.shape
    count = rows * cols
    chunks = width // LANES
    row, col = lax.axis_index("row"), lax.axis_index("col")

    sources = (
        (feat_hbm, feat), (dw_hbm, dw), (db_hbm, db), (queries_hbm, queries), (gain_hbm, gain),
        (nbias_hbm, nbias), (w1_hbm, w1), (b1_hbm, b1), (w2_hbm, w2), (b2_hbm, b2),
        (scale_hbm, scale), (wk_hbm, wkv.at[:, pl.ds(0, width)]),
        (wv_hbm, wkv.at[:, pl.ds(width, width)]), (cw_hbm, cw), (tissue_hbm, tissue),
        (label_hbm, label),
    )
    loads = [pltpu.make_async_copy(src, dst, w_sem.at[i]) for i, (src, dst) in enumerate(sources)]
    loads[0].start()

    base_row, base_col = (row // GROUP_ROWS) * GROUP_ROWS, (col // GROUP_COLS) * GROUP_COLS
    place = (row - base_row) * GROUP_COLS + (col - base_col)
    over = n_col // GROUP_COLS
    n_far = (n_row // GROUP_ROWS) * over
    far = (row // GROUP_ROWS) * over + col // GROUP_COLS

    def near_peer(step):
        other = (place + step) % GROUP
        return other, (base_row + other // GROUP_COLS, base_col + other % GROUP_COLS)

    def far_peer(step):
        other = (far + step) % n_far
        return other, (
            (other // over) * GROUP_ROWS + place // GROUP_COLS,
            (other % over) * GROUP_COLS + place % GROUP_COLS,
        )

    def present(side):
        dr, dc = side
        ok = None
        for delta, at, size in ((dr, row, n_row), (dc, col, n_col)):
            if delta:
                here = at > 0 if delta < 0 else at < size - 1
                ok = here if ok is None else jnp.logical_and(ok, here)
        return ok

    barrier = pltpu.get_barrier_semaphore()
    for side in SIDES:
        @pl.when(present(side))
        def _(side=side):
            pl.semaphore_signal(
                barrier, inc=1, device_id=(row + side[0], col + side[1]), device_id_type=MESH
            )
    for step in range(1, GROUP):
        pl.semaphore_signal(barrier, inc=1, device_id=near_peer(step)[1], device_id_type=MESH)
    for step in range(1, n_far):
        pl.semaphore_signal(barrier, inc=1, device_id=far_peer(step)[1], device_id_type=MESH)

    for load in loads[1:4]:
        load.start()
    loads[0].wait()
    stage_l[...] = feat[:, 0:8, :].astype(jnp.float32).reshape(rows * 8, width).astype(jnp.bfloat16)
    stage_r[...] = (
        feat[:, cols - 8 : cols, :].astype(jnp.float32).reshape(rows * 8, width).astype(jnp.bfloat16)
    )

    landing = {
        (-1, 0): halo_rows.at[0], (1, 0): halo_rows.at[1],
        (0, -1): halo_cols.at[0], (0, 1): halo_cols.at[1],
        (-1, -1): halo_corners.at[0], (-1, 1): halo_corners.at[1],
        (1, -1): halo_corners.at[2], (1, 1): halo_corners.at[3],
    }

    def halo_copy(side):
        dr, dc = side
        if dc == 0:
            src = feat.at[pl.ds(0, 3)] if dr < 0 else feat.at[pl.ds(rows - 3, 3)]
        else:
            src = stage_l if dc < 0 else stage_r
            if dr:
                src = src.at[pl.ds(0 if dr < 0 else rows * 8 - 32, 32)]
        return pltpu.make_async_remote_copy(
            src_ref=src,
            dst_ref=landing[(-dr, -dc)],
            send_sem=hs_sem.at[SIDES.index(side)],
            recv_sem=hr_sem.at[SIDES.index((-dr, -dc))],
            device_id=(row + dr, col + dc),
            device_id_type=MESH,
        )

    greeted = jnp.int32(GROUP - 1 + n_far - 1)
    for side in SIDES:
        greeted = greeted + present(side).astype(jnp.int32)
    pl.semaphore_wait(barrier, greeted)
    for side in SIDES:
        @pl.when(present(side))
        def _(side=side):
            halo_copy(side).start()

        @pl.when(jnp.logical_not(present(side)))
        def _(side=side):
            landing[side][...] = jnp.zeros(landing[side].shape, jnp.bfloat16)

    for load in loads[4:]:
        load.start()

    for c in range(chunks):
        lanes = slice(c * LANES, (c + 1) * LANES)
        pad[c, 3 : 3 + rows, 8 : 8 + cols, :] = feat[:, :, lanes].astype(jnp.float32)
    pad[:, 3 : 3 + rows, 0:8, :] = jnp.zeros((chunks, rows, 8, LANES), jnp.float32)
    pad[:, 3 : 3 + rows, 8 + cols :, :] = jnp.zeros((chunks, rows, 8, LANES), jnp.float32)

    loads[1].wait()
    loads[2].wait()

    def own_part(c, carry):
        at = pl.ds(pl.multiple_of(c * LANES, LANES), LANES)
        acc = [jnp.broadcast_to(db[at].reshape(1, LANES), (cols, LANES)) for _ in range(rows)]
        for b in range(7):
            taps = [dw[a, b : b + 1, at] for a in range(7)]
            for r in range(3, 3 + rows):
                window = pad[c, r, b + 5 : b + 5 + cols, :]
                for a in range(7):
                    if 0 <= r - a < rows:
                        acc[r - a] = acc[r - a] + window * taps[a]
        for i in range(rows):
            conv[c, i] = acc[i]
        return carry

    lax.fori_loop(0, chunks, own_part, 0)

    loads[3].wait()
    q32[...] = queries[...].astype(jnp.float32)
    head = lane_ids(QROWS, width) // (width // NH)
    for at, step in enumerate(ORDER):
        other = near_peer(step)[0] if step else place
        some = q32[pl.ds(pl.multiple_of(other * QROWS, QROWS), QROWS), :]
        heads = [jnp.where(head == h, some, 0.0) for h in range(NH)]
        qbig[at * NH * QROWS : (at + 1) * NH * QROWS, :] = jnp.concatenate(heads, axis=0).astype(jnp.bfloat16)

    for side in SIDES:
        @pl.when(present(side))
        def _(side=side):
            pltpu.make_async_remote_copy(
                src_ref=landing[side],
                dst_ref=landing[side],
                send_sem=hs_sem.at[SIDES.index(side)],
                recv_sem=hr_sem.at[SIDES.index(side)],
                device_id=(row + side[0], col + side[1]),
                device_id_type=MESH,
            ).wait_recv()

    for c in range(chunks):
        lanes = slice(c * LANES, (c + 1) * LANES)
        for end, first in ((0, 0), (1, 3 + rows)):
            pad[c, first : first + 3, 8 : 8 + cols, :] = halo_rows[end, :, :, lanes].astype(jnp.float32)
            for side in range(2):
                corner = halo_corners[end * 2 + side, :, lanes].astype(jnp.float32).reshape(4, 8, LANES)
                start = 0 if side == 0 else 8 + cols
                pad[c, first : first + 3, start : start + 8, :] = corner[1:4] if end == 0 else corner[0:3]
        left_pad[c, :, 0:8, :] = halo_cols[0, :, lanes].astype(jnp.float32).reshape(rows, 8, LANES)
        right_pad[c, :, 8:16, :] = halo_cols[1, :, lanes].astype(jnp.float32).reshape(rows, 8, LANES)
    left_pad[:, :, 8:16, :] = jnp.zeros((chunks, rows, 8, LANES), jnp.float32)
    right_pad[:, :, 0:8, :] = jnp.zeros((chunks, rows, 8, LANES), jnp.float32)

    def border_part(c, carry):
        at = pl.ds(pl.multiple_of(c * LANES, LANES), LANES)
        acc = [conv[c, i] for i in range(rows)]
        low = [jnp.zeros((8, LANES), jnp.float32) for _ in range(rows)]
        high = [jnp.zeros((8, LANES), jnp.float32) for _ in range(rows)]
        for b in range(7):
            taps = [dw[a, b : b + 1, at] for a in range(7)]
            for r in list(range(3)) + list(range(3 + rows, 6 + rows)):
                window = pad[c, r, b + 5 : b + 5 + cols, :]
                for a in range(7):
                    if 0 <= r - a < rows:
                        acc[r - a] = acc[r - a] + window * taps[a]
            if b != 3:
                side, edge, start = (low, left_pad, b + 5) if b < 3 else (high, right_pad, b - 3)
                for r in range(3, 3 + rows):
                    window = edge[c, r - 3, start : start + 8, :]
                    for a in range(7):
                        if 0 <= r - a < rows:
                            side[r - a] = side[r - a] + window * taps[a]
        for i in range(rows):
            conv[c, i] = acc[i]
            conv[c, i, 0:8, :] = conv[c, i, 0:8, :] + low[i]
            conv[c, i, cols - 8 : cols, :] = conv[c, i, cols - 8 : cols, :] + high[i]
        return carry

    lax.fori_loop(0, chunks, border_part, 0)

    full = jnp.concatenate([conv[c].reshape(count, LANES) for c in range(chunks)], axis=1)
    center = jnp.mean(full, axis=-1, keepdims=True)
    off = full - center
    variance = jnp.mean(off * off, axis=-1, keepdims=True)
    for load in loads[4:11]:
        load.wait()
    normed = (
        off * lax.rsqrt(variance + 1e-06) * gain[...].reshape(1, width) + nbias[...].reshape(1, width)
    ).astype(jnp.bfloat16)

    hid = w1.shape[1]
    piece = 256
    shrunk = jnp.zeros((count, width), jnp.float32)
    starts = list(range(0, hid, piece))

    def expand(start):
        part = slice(start, start + piece)
        wide = jnp.dot(normed, w1[:, part], preferred_element_type=jnp.float32)
        return wide + b1[part].reshape(1, piece)

    expanded = expand(starts[0])
    for i, start in enumerate(starts):
        following = expand(starts[i + 1]) if i + 1 < len(starts) else None
        hidden = gelu(expanded).astype(jnp.bfloat16)
        shrunk = shrunk + jnp.dot(
            hidden, w2[start : start + piece, :], preferred_element_type=jnp.float32
        )
        expanded = following
    shrunk = shrunk + b2[...].reshape(1, width)
    inputs = feat[...].astype(jnp.float32).reshape(count, width)
    block = (inputs + scale[...].reshape(1, width) * shrunk).astype(jnp.bfloat16)
    block_ref[...] = block.reshape(rows, cols, width)

    for load in loads[11:]:
        load.wait()
    both = jnp.dot(block, wkv[...], preferred_element_type=jnp.float32).astype(jnp.bfloat16)
    keys, values = both[:, :width], both[:, width:]
    cell = lane_ids(1, count)
    tile = (cell // cols) // TILE * (cols // TILE) + (cell % cols) // TILE
    alive = jnp.zeros((1, count), jnp.int32)
    for i in range(rows // TILE):
        for j in range(cols // TILE):
            alive = jnp.where(tile == i * (cols // TILE) + j, tissue[i, j], alive)
    live = alive > 0
    lane = lane_ids(QROWS, LANES)
    copies_a = []
    per_call = GROUP // CALLS
    size = NH * QROWS
    for call in range(CALLS):
        scores = lax.dot_general(
            qbig[call * per_call * size : (call + 1) * per_call * size, :], keys,
            (((1,), (1,)), ((), ())), preferred_element_type=jnp.float32,
        ) * (width // NH) ** (-0.5)
        scores = jnp.where(live, scores, -1e30)
        peak = jnp.max(scores, axis=1, keepdims=True)
        weights = jnp.where(live, jnp.exp(scores - peak), 0.0)
        total = jnp.sum(weights, axis=1, keepdims=True)
        mixed = jnp.dot(weights.astype(jnp.bfloat16), values, preferred_element_type=jnp.float32)
        for i in range(per_call):
            at = call * per_call + i
            weighted = jnp.zeros((QROWS, width), jnp.float32)
            tail = jnp.zeros((QROWS, LANES), jnp.float32)
            for h in range(NH):
                own = slice(i * size + h * QROWS, i * size + (h + 1) * QROWS)
                weighted = jnp.where(head == h, mixed[own], weighted)
                tail = jnp.where(lane == h, peak[own], tail)
                tail = jnp.where(lane == NH + h, total[own], tail)
            step = ORDER[at]
            if step == 0:
                got_a[place, :, :width] = weighted
                got_a[place, :, width:] = tail
                continue
            msg[at, :, :width] = weighted
            msg[at, :, width:] = tail
            copies_a.append(pltpu.make_async_remote_copy(
                src_ref=msg.at[at],
                dst_ref=got_a.at[place],
                send_sem=as_sem.at[step],
                recv_sem=ar_sem.at[place],
                device_id=near_peer(step)[1],
                device_id_type=MESH,
            ))
            copies_a[-1].start()

    def arrival(dst, sem):
        return pltpu.make_async_remote_copy(
            src_ref=dst, dst_ref=dst, send_sem=as_sem.at[0], recv_sem=sem,
            device_id=near_peer(1)[1], device_id_type=MESH,
        )

    for step in range(1, GROUP):
        other = near_peer(step)[0]
        arrival(got_a.at[other], ar_sem.at[other]).wait_recv()
    weighted, tail = combine(got_a, GROUP, width)

    if n_far > 1:
        mine[:, :width] = weighted
        mine[:, width:] = tail
        copies_b = []
        for step in range(1, n_far):
            other, device = far_peer(step)
            copies_b.append(pltpu.make_async_remote_copy(
                src_ref=mine,
                dst_ref=got_b.at[far],
                send_sem=bs_sem.at[step],
                recv_sem=br_sem.at[far],
                device_id=device,
                device_id_type=MESH,
            ))
            copies_b[-1].start()
        got_b[far] = mine[...]
        for step in range(1, n_far):
            other = far_peer(step)[0]
            arrival(got_b.at[other], br_sem.at[other]).wait_recv()
        weighted, tail = combine(got_b, n_far, width)
    pooled[place] = weighted / spread(tail, NH, width)

    copies_c = []
    for step in range(1, GROUP):
        other, device = near_peer(step)
        copies_c.append(pltpu.make_async_remote_copy(
            src_ref=pooled.at[place],
            dst_ref=pooled.at[place],
            send_sem=cs_sem.at[step],
            recv_sem=cr_sem.at[place],
            device_id=device,
            device_id_type=MESH,
        ))
        copies_c[-1].start()
    for step in range(1, GROUP):
        other = near_peer(step)[0]
        arrival(pooled.at[other], cr_sem.at[other]).wait_recv()
    result = pooled[...].reshape(NQ, width)
    pooled_ref[...] = result
    summed = jnp.sum(result, axis=0, keepdims=True)
    logits = jnp.sum(summed * cw[...], axis=1, keepdims=True)
    soft = jnp.maximum(logits, 0.0) + jnp.log1p(jnp.exp(-jnp.abs(logits)))
    n_lab = cw.shape[0]
    which = lax.broadcasted_iota(jnp.int32, (n_lab, 1), 0)
    truth = jnp.zeros((n_lab, 1), jnp.int32)
    for k in range(n_lab):
        truth = jnp.where(which == k, label[k], truth)
    loss_ref[0] = jnp.sum(soft - truth.astype(jnp.float32) * logits)

    for side in SIDES:
        @pl.when(present(side))
        def _(side=side):
            halo_copy(side).wait_send()
    for copy in copies_a:
        copy.wait_send()
    if n_far > 1:
        for copy in copies_b:
            copy.wait_send()
    for copy in copies_c:
        copy.wait_send()


def per_device(
    n_row, n_col,
    features, depth_weight, depth_bias, norm_gain, norm_bias, expand_weight, expand_bias,
    shrink_weight, shrink_bias, layer_scale, key_weight, value_weight, queries, class_weight,
    tissue, slide_label,
):
    rows, cols, width = features.shape
    hid = expand_weight.shape[1]
    chunks = width // LANES
    n_far = (n_row // GROUP_ROWS) * (n_col // GROUP_COLS)
    vmem = pl.BlockSpec(memory_space=pltpu.VMEM)
    smem = pl.BlockSpec(memory_space=pltpu.SMEM)
    hbm = pl.BlockSpec(memory_space=pltpu.HBM)
    wide = width + LANES
    f32, bf16 = jnp.float32, jnp.bfloat16
    dma = pltpu.SemaphoreType.DMA
    block, pooled, loss = pl.pallas_call(
        functools.partial(kernel, n_row, n_col),
        out_shape=(
            pltpu.VMEM((rows, cols, width), bf16),
            pltpu.VMEM((NQ, width), f32),
            jax.ShapeDtypeStruct((1,), f32),
        ),
        in_specs=[hbm] * 16,
        out_specs=(vmem, vmem, smem),
        scratch_shapes=[
            pltpu.VMEM((rows, cols, width), bf16),
            pltpu.VMEM(depth_weight.shape, f32),
            pltpu.VMEM((width,), f32),
            pltpu.VMEM((width,), f32),
            pltpu.VMEM((width,), f32),
            pltpu.VMEM((width, hid), bf16),
            pltpu.VMEM((hid,), f32),
            pltpu.VMEM((hid, width), bf16),
            pltpu.VMEM((width,), f32),
            pltpu.VMEM((width,), f32),
            pltpu.VMEM((width, 2 * width), bf16),
            pltpu.VMEM((NQ, width), bf16),
            pltpu.VMEM((class_weight.shape[1], width), f32),
            pltpu.SMEM(tissue.shape, jnp.int32),
            pltpu.SMEM(slide_label.shape, jnp.int32),
            pltpu.VMEM((NQ, width), f32),
            pltpu.VMEM((chunks, rows + 6, cols + 16, LANES), f32),
            pltpu.VMEM((chunks, rows, 16, LANES), f32),
            pltpu.VMEM((chunks, rows, 16, LANES), f32),
            pltpu.VMEM((chunks, rows, cols, LANES), f32),
            pltpu.VMEM((NH * NQ, width), bf16),
            pltpu.VMEM((rows * 8, width), bf16),
            pltpu.VMEM((rows * 8, width), bf16),
            pltpu.VMEM((2, 3, cols, width), bf16),
            pltpu.VMEM((2, rows * 8, width), bf16),
            pltpu.VMEM((4, 32, width), bf16),
            pltpu.VMEM((GROUP, QROWS, wide), f32),
            pltpu.VMEM((GROUP, QROWS, wide), f32),
            pltpu.VMEM((n_far, QROWS, wide), f32),
            pltpu.VMEM((QROWS, wide), f32),
            pltpu.VMEM((GROUP, QROWS, width), f32),
            dma((16,)),
            dma((8,)),
            dma((8,)),
            dma((GROUP,)),
            dma((GROUP,)),
            dma((n_far,)),
            dma((n_far,)),
            dma((GROUP,)),
            dma((GROUP,)),
        ],
        compiler_params=pltpu.CompilerParams(
            collective_id=0, has_side_effects=True, vmem_limit_bytes=63 * 1024 * 1024
        ),
    )(
        features, depth_weight, depth_bias, norm_gain, norm_bias, expand_weight, expand_bias,
        shrink_weight, shrink_bias, layer_scale, key_weight, value_weight, queries, class_weight.T,
        tissue, slide_label,
    )
    return block, pooled, loss


def solution(mesh):
    everywhere = P()
    cells = P("row", "col", None)
    placed = (cells,) + (everywhere,) * 13 + (P("row", "col"), everywhere)
    return jax.shard_map(
        functools.partial(per_device, mesh.shape["row"], mesh.shape["col"]),
        mesh=mesh,
        in_specs=placed,
        out_specs=(cells, everywhere, everywhere),
        check_vma=False,
    )
```

```python
import functools

import jax
import jax.numpy as jnp
from jax import lax
from jax.experimental import pallas as pl
from jax.experimental.pallas import tpu as pltpu
from jax.sharding import PartitionSpec as P

NH = 8
NQ = 64
TILE = 8
LANES = 128
GROUP_ROWS, GROUP_COLS = 4, 2
GROUP = GROUP_ROWS * GROUP_COLS
QROWS = NQ // GROUP
ORDER = (4, 5, 6, 7, 1, 2, 3, 0)
CALLS = 2
MESH = pl.DeviceIdType.MESH
SIDES = [(-1, 0), (1, 0), (0, -1), (0, 1), (-1, -1), (-1, 1), (1, -1), (1, 1)]


def lane_ids(rows, width):
    return lax.broadcasted_iota(jnp.int32, (rows, width), 1)


def spread(cols, first, width):
    rows = cols.shape[0]
    head = lane_ids(rows, width) // (width // NH)
    out = jnp.zeros((rows, width), jnp.float32)
    for h in range(NH):
        out = jnp.where(head == h, cols[:, first + h : first + h + 1], out)
    return out


def combine(ref, count, width):
    tails = [ref[s, :, width:] for s in range(count)]
    peak = functools.reduce(jnp.maximum, tails)
    weighted = jnp.zeros((QROWS, width), jnp.float32)
    total = jnp.zeros((QROWS, LANES), jnp.float32)
    for s in range(count):
        factor = jnp.exp(tails[s] - peak)
        total = total + pltpu.roll(factor, NH, 1) * tails[s]
        weighted = weighted + ref[s, :, :width] * spread(factor, 0, width)
    return weighted, jnp.where(lane_ids(QROWS, LANES) < NH, peak, total)


def kernel(
    n_row, n_col,
    feat_hbm, dw_hbm, db_hbm, gain_hbm, nbias_hbm, w1_hbm, b1_hbm, w2_hbm, b2_hbm, scale_hbm,
    wk_hbm, wv_hbm, queries_hbm, cw_hbm, tissue_hbm, label_hbm,
    block_ref, pooled_ref, loss_ref,
    feat, dw, db, gain, nbias, w1, b1, w2, b2, scale, wkv, queries, cw, tissue, label, q32, pad, left_pad, right_pad, conv, qbig,
    stage_l, stage_r, halo_rows, halo_cols, halo_corners, msg, got_a, got_b, mine, pooled,
    w_sem, hs_sem, hr_sem, as_sem, ar_sem, bs_sem, br_sem, cs_sem, cr_sem,
):
    rows, cols, width = feat_hbm.shape
    count = rows * cols
    chunks = width // LANES
    row, col = lax.axis_index("row"), lax.axis_index("col")

    sources = (
        (feat_hbm, feat), (dw_hbm, dw), (db_hbm, db), (queries_hbm, queries), (gain_hbm, gain),
        (nbias_hbm, nbias), (w1_hbm, w1), (b1_hbm, b1), (w2_hbm, w2), (b2_hbm, b2),
        (scale_hbm, scale), (wk_hbm, wkv.at[:, pl.ds(0, width)]),
        (wv_hbm, wkv.at[:, pl.ds(width, width)]), (cw_hbm, cw), (tissue_hbm, tissue),
        (label_hbm, label),
    )
    loads = [pltpu.make_async_copy(src, dst, w_sem.at[i]) for i, (src, dst) in enumerate(sources)]
    loads[0].start()

    base_row, base_col = (row // GROUP_ROWS) * GROUP_ROWS, (col // GROUP_COLS) * GROUP_COLS
    place = (row - base_row) * GROUP_COLS + (col - base_col)
    over = n_col // GROUP_COLS
    n_far = (n_row // GROUP_ROWS) * over
    far = (row // GROUP_ROWS) * over + col // GROUP_COLS

    def near_peer(step):
        other = (place + step) % GROUP
        return other, (base_row + other // GROUP_COLS, base_col + other % GROUP_COLS)

    def far_peer(step):
        other = (far + step) % n_far
        return other, (
            (other // over) * GROUP_ROWS + place // GROUP_COLS,
            (other % over) * GROUP_COLS + place % GROUP_COLS,
        )

    def present(side):
        dr, dc = side
        ok = None
        for delta, at, size in ((dr, row, n_row), (dc, col, n_col)):
            if delta:
                here = at > 0 if delta < 0 else at < size - 1
                ok = here if ok is None else jnp.logical_and(ok, here)
        return ok

    barrier = pltpu.get_barrier_semaphore()
    for side in SIDES:
        @pl.when(present(side))
        def _(side=side):
            pl.semaphore_signal(
                barrier, inc=1, device_id=(row + side[0], col + side[1]), device_id_type=MESH
            )
    for step in range(1, GROUP):
        pl.semaphore_signal(barrier, inc=1, device_id=near_peer(step)[1], device_id_type=MESH)
    for step in range(1, n_far):
        pl.semaphore_signal(barrier, inc=1, device_id=far_peer(step)[1], device_id_type=MESH)

    for load in loads[1:]:
        load.start()
    loads[0].wait()
    stage_l[...] = feat[:, 0:8, :].astype(jnp.float32).reshape(rows * 8, width).astype(jnp.bfloat16)
    stage_r[...] = (
        feat[:, cols - 8 : cols, :].astype(jnp.float32).reshape(rows * 8, width).astype(jnp.bfloat16)
    )

    landing = {
        (-1, 0): halo_rows.at[0], (1, 0): halo_rows.at[1],
        (0, -1): halo_cols.at[0], (0, 1): halo_cols.at[1],
        (-1, -1): halo_corners.at[0], (-1, 1): halo_corners.at[1],
        (1, -1): halo_corners.at[2], (1, 1): halo_corners.at[3],
    }

    def halo_copy(side):
        dr, dc = side
        if dc == 0:
            src = feat.at[pl.ds(0, 3)] if dr < 0 else feat.at[pl.ds(rows - 3, 3)]
        else:
            src = stage_l if dc < 0 else stage_r
            if dr:
                src = src.at[pl.ds(0 if dr < 0 else rows * 8 - 32, 32)]
        return pltpu.make_async_remote_copy(
            src_ref=src,
            dst_ref=landing[(-dr, -dc)],
            send_sem=hs_sem.at[SIDES.index(side)],
            recv_sem=hr_sem.at[SIDES.index((-dr, -dc))],
            device_id=(row + dr, col + dc),
            device_id_type=MESH,
        )

    greeted = jnp.int32(GROUP - 1 + n_far - 1)
    for side in SIDES:
        greeted = greeted + present(side).astype(jnp.int32)
    pl.semaphore_wait(barrier, greeted)
    for side in SIDES:
        @pl.when(present(side))
        def _(side=side):
            halo_copy(side).start()

        @pl.when(jnp.logical_not(present(side)))
        def _(side=side):
            landing[side][...] = jnp.zeros(landing[side].shape, jnp.bfloat16)

    for c in range(chunks):
        lanes = slice(c * LANES, (c + 1) * LANES)
        pad[c, 3 : 3 + rows, 8 : 8 + cols, :] = feat[:, :, lanes].astype(jnp.float32)
    pad[:, 3 : 3 + rows, 0:8, :] = jnp.zeros((chunks, rows, 8, LANES), jnp.float32)
    pad[:, 3 : 3 + rows, 8 + cols :, :] = jnp.zeros((chunks, rows, 8, LANES), jnp.float32)

    loads[1].wait()
    loads[2].wait()

    def own_part(c, carry):
        at = pl.ds(pl.multiple_of(c * LANES, LANES), LANES)
        acc = [jnp.broadcast_to(db[at].reshape(1, LANES), (cols, LANES)) for _ in range(rows)]
        for b in range(7):
            taps = [dw[a, b : b + 1, at] for a in range(7)]
            for r in range(3, 3 + rows):
                window = pad[c, r, b + 5 : b + 5 + cols, :]
                for a in range(7):
                    if 0 <= r - a < rows:
                        acc[r - a] = acc[r - a] + window * taps[a]
        for i in range(rows):
            conv[c, i] = acc[i]
        return carry

    lax.fori_loop(0, chunks, own_part, 0)

    loads[3].wait()
    q32[...] = queries[...].astype(jnp.float32)
    head = lane_ids(QROWS, width) // (width // NH)
    for at, step in enumerate(ORDER):
        other = near_peer(step)[0] if step else place
        some = q32[pl.ds(pl.multiple_of(other * QROWS, QROWS), QROWS), :]
        heads = [jnp.where(head == h, some, 0.0) for h in range(NH)]
        qbig[at * NH * QROWS : (at + 1) * NH * QROWS, :] = jnp.concatenate(heads, axis=0).astype(jnp.bfloat16)

    for side in SIDES:
        @pl.when(present(side))
        def _(side=side):
            pltpu.make_async_remote_copy(
                src_ref=landing[side],
                dst_ref=landing[side],
                send_sem=hs_sem.at[SIDES.index(side)],
                recv_sem=hr_sem.at[SIDES.index(side)],
                device_id=(row + side[0], col + side[1]),
                device_id_type=MESH,
            ).wait_recv()

    for c in range(chunks):
        lanes = slice(c * LANES, (c + 1) * LANES)
        for end, first in ((0, 0), (1, 3 + rows)):
            pad[c, first : first + 3, 8 : 8 + cols, :] = halo_rows[end, :, :, lanes].astype(jnp.float32)
            for side in range(2):
                corner = halo_corners[end * 2 + side, :, lanes].astype(jnp.float32).reshape(4, 8, LANES)
                start = 0 if side == 0 else 8 + cols
                pad[c, first : first + 3, start : start + 8, :] = corner[1:4] if end == 0 else corner[0:3]
        left_pad[c, :, 0:8, :] = halo_cols[0, :, lanes].astype(jnp.float32).reshape(rows, 8, LANES)
        right_pad[c, :, 8:16, :] = halo_cols[1, :, lanes].astype(jnp.float32).reshape(rows, 8, LANES)
    left_pad[:, :, 8:16, :] = jnp.zeros((chunks, rows, 8, LANES), jnp.float32)
    right_pad[:, :, 0:8, :] = jnp.zeros((chunks, rows, 8, LANES), jnp.float32)

    def border_part(c, carry):
        at = pl.ds(pl.multiple_of(c * LANES, LANES), LANES)
        acc = [conv[c, i] for i in range(rows)]
        low = [jnp.zeros((8, LANES), jnp.float32) for _ in range(rows)]
        high = [jnp.zeros((8, LANES), jnp.float32) for _ in range(rows)]
        for b in range(7):
            taps = [dw[a, b : b + 1, at] for a in range(7)]
            for r in list(range(3)) + list(range(3 + rows, 6 + rows)):
                window = pad[c, r, b + 5 : b + 5 + cols, :]
                for a in range(7):
                    if 0 <= r - a < rows:
                        acc[r - a] = acc[r - a] + window * taps[a]
            if b != 3:
                side, edge, start = (low, left_pad, b + 5) if b < 3 else (high, right_pad, b - 3)
                for r in range(3, 3 + rows):
                    window = edge[c, r - 3, start : start + 8, :]
                    for a in range(7):
                        if 0 <= r - a < rows:
                            side[r - a] = side[r - a] + window * taps[a]
        for i in range(rows):
            conv[c, i] = acc[i]
            conv[c, i, 0:8, :] = conv[c, i, 0:8, :] + low[i]
            conv[c, i, cols - 8 : cols, :] = conv[c, i, cols - 8 : cols, :] + high[i]
        return carry

    lax.fori_loop(0, chunks, border_part, 0)

    full = jnp.concatenate([conv[c].reshape(count, LANES) for c in range(chunks)], axis=1)
    center = jnp.mean(full, axis=-1, keepdims=True)
    off = full - center
    variance = jnp.mean(off * off, axis=-1, keepdims=True)
    for load in loads[4:11]:
        load.wait()
    normed = (
        off * lax.rsqrt(variance + 1e-06) * gain[...].reshape(1, width) + nbias[...].reshape(1, width)
    ).astype(jnp.bfloat16)

    hid = w1.shape[1]
    piece = 256
    shrunk = jnp.zeros((count, width), jnp.float32)
    starts = list(range(0, hid, piece))

    def expand(start):
        part = slice(start, start + piece)
        wide = jnp.dot(normed, w1[:, part], preferred_element_type=jnp.float32)
        return wide + b1[part].reshape(1, piece)

    expanded = expand(starts[0])
    for i, start in enumerate(starts):
        following = expand(starts[i + 1]) if i + 1 < len(starts) else None
        hidden = (0.5 * expanded * (1.0 + lax.erf(expanded * 0.5**0.5))).astype(jnp.bfloat16)
        shrunk = shrunk + jnp.dot(
            hidden, w2[start : start + piece, :], preferred_element_type=jnp.float32
        )
        expanded = following
    shrunk = shrunk + b2[...].reshape(1, width)
    inputs = feat[...].astype(jnp.float32).reshape(count, width)
    block = (inputs + scale[...].reshape(1, width) * shrunk).astype(jnp.bfloat16)
    block_ref[...] = block.reshape(rows, cols, width)

    for load in loads[11:]:
        load.wait()
    both = jnp.dot(block, wkv[...], preferred_element_type=jnp.float32).astype(jnp.bfloat16)
    keys, values = both[:, :width], both[:, width:]
    cell = lane_ids(1, count)
    tile = (cell // cols) // TILE * (cols // TILE) + (cell % cols) // TILE
    alive = jnp.zeros((1, count), jnp.int32)
    for i in range(rows // TILE):
        for j in range(cols // TILE):
            alive = jnp.where(tile == i * (cols // TILE) + j, tissue[i, j], alive)
    live = alive > 0
    lane = lane_ids(QROWS, LANES)
    copies_a = []
    per_call = GROUP // CALLS
    size = NH * QROWS
    for call in range(CALLS):
        scores = lax.dot_general(
            qbig[call * per_call * size : (call + 1) * per_call * size, :], keys,
            (((1,), (1,)), ((), ())), preferred_element_type=jnp.float32,
        ) * (width // NH) ** (-0.5)
        scores = jnp.where(live, scores, -1e30)
        peak = jnp.max(scores, axis=1, keepdims=True)
        weights = jnp.where(live, jnp.exp(scores - peak), 0.0)
        total = jnp.sum(weights, axis=1, keepdims=True)
        mixed = jnp.dot(weights.astype(jnp.bfloat16), values, preferred_element_type=jnp.float32)
        for i in range(per_call):
            at = call * per_call + i
            weighted = jnp.zeros((QROWS, width), jnp.float32)
            tail = jnp.zeros((QROWS, LANES), jnp.float32)
            for h in range(NH):
                own = slice(i * size + h * QROWS, i * size + (h + 1) * QROWS)
                weighted = jnp.where(head == h, mixed[own], weighted)
                tail = jnp.where(lane == h, peak[own], tail)
                tail = jnp.where(lane == NH + h, total[own], tail)
            step = ORDER[at]
            if step == 0:
                got_a[place, :, :width] = weighted
                got_a[place, :, width:] = tail
                continue
            msg[at, :, :width] = weighted
            msg[at, :, width:] = tail
            copies_a.append(pltpu.make_async_remote_copy(
                src_ref=msg.at[at],
                dst_ref=got_a.at[place],
                send_sem=as_sem.at[step],
                recv_sem=ar_sem.at[place],
                device_id=near_peer(step)[1],
                device_id_type=MESH,
            ))
            copies_a[-1].start()

    def arrival(dst, sem):
        return pltpu.make_async_remote_copy(
            src_ref=dst, dst_ref=dst, send_sem=as_sem.at[0], recv_sem=sem,
            device_id=near_peer(1)[1], device_id_type=MESH,
        )

    for step in range(1, GROUP):
        other = near_peer(step)[0]
        arrival(got_a.at[other], ar_sem.at[other]).wait_recv()
    weighted, tail = combine(got_a, GROUP, width)

    if n_far > 1:
        mine[:, :width] = weighted
        mine[:, width:] = tail
        copies_b = []
        for step in range(1, n_far):
            other, device = far_peer(step)
            copies_b.append(pltpu.make_async_remote_copy(
                src_ref=mine,
                dst_ref=got_b.at[far],
                send_sem=bs_sem.at[step],
                recv_sem=br_sem.at[far],
                device_id=device,
                device_id_type=MESH,
            ))
            copies_b[-1].start()
        got_b[far] = mine[...]
        for step in range(1, n_far):
            other = far_peer(step)[0]
            arrival(got_b.at[other], br_sem.at[other]).wait_recv()
        weighted, tail = combine(got_b, n_far, width)
    pooled[place] = weighted / spread(tail, NH, width)

    copies_c = []
    for step in range(1, GROUP):
        other, device = near_peer(step)
        copies_c.append(pltpu.make_async_remote_copy(
            src_ref=pooled.at[place],
            dst_ref=pooled.at[place],
            send_sem=cs_sem.at[step],
            recv_sem=cr_sem.at[place],
            device_id=device,
            device_id_type=MESH,
        ))
        copies_c[-1].start()
    for step in range(1, GROUP):
        other = near_peer(step)[0]
        arrival(pooled.at[other], cr_sem.at[other]).wait_recv()
    result = pooled[...].reshape(NQ, width)
    pooled_ref[...] = result
    summed = jnp.sum(result, axis=0, keepdims=True)
    logits = jnp.sum(summed * cw[...], axis=1, keepdims=True)
    soft = jnp.maximum(logits, 0.0) + jnp.log1p(jnp.exp(-jnp.abs(logits)))
    n_lab = cw.shape[0]
    which = lax.broadcasted_iota(jnp.int32, (n_lab, 1), 0)
    truth = jnp.zeros((n_lab, 1), jnp.int32)
    for k in range(n_lab):
        truth = jnp.where(which == k, label[k], truth)
    loss_ref[0] = jnp.sum(soft - truth.astype(jnp.float32) * logits)

    for side in SIDES:
        @pl.when(present(side))
        def _(side=side):
            halo_copy(side).wait_send()
    for copy in copies_a:
        copy.wait_send()
    if n_far > 1:
        for copy in copies_b:
            copy.wait_send()
    for copy in copies_c:
        copy.wait_send()


def per_device(
    n_row, n_col,
    features, depth_weight, depth_bias, norm_gain, norm_bias, expand_weight, expand_bias,
    shrink_weight, shrink_bias, layer_scale, key_weight, value_weight, queries, class_weight,
    tissue, slide_label,
):
    rows, cols, width = features.shape
    hid = expand_weight.shape[1]
    chunks = width // LANES
    n_far = (n_row // GROUP_ROWS) * (n_col // GROUP_COLS)
    vmem = pl.BlockSpec(memory_space=pltpu.VMEM)
    smem = pl.BlockSpec(memory_space=pltpu.SMEM)
    hbm = pl.BlockSpec(memory_space=pltpu.HBM)
    wide = width + LANES
    f32, bf16 = jnp.float32, jnp.bfloat16
    dma = pltpu.SemaphoreType.DMA
    block, pooled, loss = pl.pallas_call(
        functools.partial(kernel, n_row, n_col),
        out_shape=(
            pltpu.VMEM((rows, cols, width), bf16),
            pltpu.VMEM((NQ, width), f32),
            jax.ShapeDtypeStruct((1,), f32),
        ),
        in_specs=[hbm] * 16,
        out_specs=(vmem, vmem, smem),
        scratch_shapes=[
            pltpu.VMEM((rows, cols, width), bf16),
            pltpu.VMEM(depth_weight.shape, f32),
            pltpu.VMEM((width,), f32),
            pltpu.VMEM((width,), f32),
            pltpu.VMEM((width,), f32),
            pltpu.VMEM((width, hid), bf16),
            pltpu.VMEM((hid,), f32),
            pltpu.VMEM((hid, width), bf16),
            pltpu.VMEM((width,), f32),
            pltpu.VMEM((width,), f32),
            pltpu.VMEM((width, 2 * width), bf16),
            pltpu.VMEM((NQ, width), bf16),
            pltpu.VMEM((class_weight.shape[1], width), f32),
            pltpu.SMEM(tissue.shape, jnp.int32),
            pltpu.SMEM(slide_label.shape, jnp.int32),
            pltpu.VMEM((NQ, width), f32),
            pltpu.VMEM((chunks, rows + 6, cols + 16, LANES), f32),
            pltpu.VMEM((chunks, rows, 16, LANES), f32),
            pltpu.VMEM((chunks, rows, 16, LANES), f32),
            pltpu.VMEM((chunks, rows, cols, LANES), f32),
            pltpu.VMEM((NH * NQ, width), bf16),
            pltpu.VMEM((rows * 8, width), bf16),
            pltpu.VMEM((rows * 8, width), bf16),
            pltpu.VMEM((2, 3, cols, width), bf16),
            pltpu.VMEM((2, rows * 8, width), bf16),
            pltpu.VMEM((4, 32, width), bf16),
            pltpu.VMEM((GROUP, QROWS, wide), f32),
            pltpu.VMEM((GROUP, QROWS, wide), f32),
            pltpu.VMEM((n_far, QROWS, wide), f32),
            pltpu.VMEM((QROWS, wide), f32),
            pltpu.VMEM((GROUP, QROWS, width), f32),
            dma((16,)),
            dma((8,)),
            dma((8,)),
            dma((GROUP,)),
            dma((GROUP,)),
            dma((n_far,)),
            dma((n_far,)),
            dma((GROUP,)),
            dma((GROUP,)),
        ],
        compiler_params=pltpu.CompilerParams(
            collective_id=0, has_side_effects=True, vmem_limit_bytes=63 * 1024 * 1024
        ),
    )(
        features, depth_weight, depth_bias, norm_gain, norm_bias, expand_weight, expand_bias,
        shrink_weight, shrink_bias, layer_scale, key_weight, value_weight, queries, class_weight.T,
        tissue, slide_label,
    )
    return block, pooled, loss


def solution(mesh):
    everywhere = P()
    cells = P("row", "col", None)
    placed = (cells,) + (everywhere,) * 13 + (P("row", "col"), everywhere)
    return jax.shard_map(
        functools.partial(per_device, mesh.shape["row"], mesh.shape["col"]),
        mesh=mesh,
        in_specs=placed,
        out_specs=(cells, everywhere, everywhere),
        check_vma=False,
    )
```

```python
import functools

import jax
import jax.numpy as jnp
from jax import lax
from jax.experimental import pallas as pl
from jax.experimental.pallas import tpu as pltpu
from jax.sharding import PartitionSpec as P

NH = 8
NQ = 64
TILE = 8
LANES = 128
GROUP_ROWS, GROUP_COLS = 4, 2
GROUP = GROUP_ROWS * GROUP_COLS
QROWS = NQ // GROUP
ORDER = (7, 5, 6, 4, 3, 1, 2, 0)
CALLS = 2
MESH = pl.DeviceIdType.MESH
SIDES = [(-1, 0), (1, 0), (0, -1), (0, 1), (-1, -1), (-1, 1), (1, -1), (1, 1)]


def lane_ids(rows, width):
    return lax.broadcasted_iota(jnp.int32, (rows, width), 1)


def spread(cols, first, width):
    rows = cols.shape[0]
    head = lane_ids(rows, width) // (width // NH)
    out = jnp.zeros((rows, width), jnp.float32)
    for h in range(NH):
        out = jnp.where(head == h, cols[:, first + h : first + h + 1], out)
    return out


def combine(ref, count, width):
    tails = [ref[s, :, width:] for s in range(count)]
    peak = functools.reduce(jnp.maximum, tails)
    weighted = jnp.zeros((QROWS, width), jnp.float32)
    total = jnp.zeros((QROWS, LANES), jnp.float32)
    for s in range(count):
        factor = jnp.exp(tails[s] - peak)
        total = total + pltpu.roll(factor, NH, 1) * tails[s]
        weighted = weighted + ref[s, :, :width] * spread(factor, 0, width)
    return weighted, jnp.where(lane_ids(QROWS, LANES) < NH, peak, total)


def kernel(
    n_row, n_col,
    feat_hbm, dw_hbm, db_hbm, gain_hbm, nbias_hbm, w1_hbm, b1_hbm, w2_hbm, b2_hbm, scale_hbm,
    wk_hbm, wv_hbm, queries_hbm, cw_hbm, tissue_hbm, label_hbm,
    block_ref, pooled_ref, loss_ref,
    feat, dw, db, gain, nbias, w1, b1, w2, b2, scale, wkv, queries, cw, tissue, label, q32, pad, left_pad, right_pad, conv, qbig,
    stage_l, stage_r, halo_rows, halo_cols, halo_corners, msg, got_a, got_b, mine, pooled,
    w_sem, hs_sem, hr_sem, as_sem, ar_sem, bs_sem, br_sem, cs_sem, cr_sem,
):
    rows, cols, width = feat_hbm.shape
    count = rows * cols
    chunks = width // LANES
    row, col = lax.axis_index("row"), lax.axis_index("col")

    sources = (
        (feat_hbm, feat), (dw_hbm, dw), (db_hbm, db), (queries_hbm, queries), (gain_hbm, gain),
        (nbias_hbm, nbias), (w1_hbm, w1), (b1_hbm, b1), (w2_hbm, w2), (b2_hbm, b2),
        (scale_hbm, scale), (wk_hbm, wkv.at[:, pl.ds(0, width)]),
        (wv_hbm, wkv.at[:, pl.ds(width, width)]), (cw_hbm, cw), (tissue_hbm, tissue),
        (label_hbm, label),
    )
    loads = [pltpu.make_async_copy(src, dst, w_sem.at[i]) for i, (src, dst) in enumerate(sources)]
    loads[0].start()

    base_row, base_col = (row // GROUP_ROWS) * GROUP_ROWS, (col // GROUP_COLS) * GROUP_COLS
    place = (row - base_row) * GROUP_COLS + (col - base_col)
    over = n_col // GROUP_COLS
    n_far = (n_row // GROUP_ROWS) * over
    far = (row // GROUP_ROWS) * over + col // GROUP_COLS

    def near_peer(step):
        other = (
            (place // 4 + step // 4) % 2 * 4
            + (place // 2 + step // 2) % 2 * 2
            + (place + step) % 2
        )
        return other, (base_row + other // GROUP_COLS, base_col + other % GROUP_COLS)

    def far_peer(step):
        other = (far + step) % n_far
        return other, (
            (other // over) * GROUP_ROWS + place // GROUP_COLS,
            (other % over) * GROUP_COLS + place % GROUP_COLS,
        )

    def present(side):
        dr, dc = side
        ok = None
        for delta, at, size in ((dr, row, n_row), (dc, col, n_col)):
            if delta:
                here = at > 0 if delta < 0 else at < size - 1
                ok = here if ok is None else jnp.logical_and(ok, here)
        return ok

    barrier = pltpu.get_barrier_semaphore()
    for side in SIDES:
        @pl.when(present(side))
        def _(side=side):
            pl.semaphore_signal(
                barrier, inc=1, device_id=(row + side[0], col + side[1]), device_id_type=MESH
            )
    for step in range(1, GROUP):
        pl.semaphore_signal(barrier, inc=1, device_id=near_peer(step)[1], device_id_type=MESH)
    for step in range(1, n_far):
        pl.semaphore_signal(barrier, inc=1, device_id=far_peer(step)[1], device_id_type=MESH)

    for load in loads[1:]:
        load.start()
    loads[0].wait()
    stage_l[...] = feat[:, 0:8, :].astype(jnp.float32).reshape(rows * 8, width).astype(jnp.bfloat16)
    stage_r[...] = (
        feat[:, cols - 8 : cols, :].astype(jnp.float32).reshape(rows * 8, width).astype(jnp.bfloat16)
    )

    landing = {
        (-1, 0): halo_rows.at[0], (1, 0): halo_rows.at[1],
        (0, -1): halo_cols.at[0], (0, 1): halo_cols.at[1],
        (-1, -1): halo_corners.at[0], (-1, 1): halo_corners.at[1],
        (1, -1): halo_corners.at[2], (1, 1): halo_corners.at[3],
    }

    def halo_copy(side):
        dr, dc = side
        if dc == 0:
            src = feat.at[pl.ds(0, 3)] if dr < 0 else feat.at[pl.ds(rows - 3, 3)]
        else:
            src = stage_l if dc < 0 else stage_r
            if dr:
                src = src.at[pl.ds(0 if dr < 0 else rows * 8 - 32, 32)]
        return pltpu.make_async_remote_copy(
            src_ref=src,
            dst_ref=landing[(-dr, -dc)],
            send_sem=hs_sem.at[SIDES.index(side)],
            recv_sem=hr_sem.at[SIDES.index((-dr, -dc))],
            device_id=(row + dr, col + dc),
            device_id_type=MESH,
        )

    greeted = jnp.int32(GROUP - 1 + n_far - 1)
    for side in SIDES:
        greeted = greeted + present(side).astype(jnp.int32)
    pl.semaphore_wait(barrier, greeted)
    for side in SIDES:
        @pl.when(present(side))
        def _(side=side):
            halo_copy(side).start()

        @pl.when(jnp.logical_not(present(side)))
        def _(side=side):
            landing[side][...] = jnp.zeros(landing[side].shape, jnp.bfloat16)

    for c in range(chunks):
        lanes = slice(c * LANES, (c + 1) * LANES)
        pad[c, 3 : 3 + rows, 8 : 8 + cols, :] = feat[:, :, lanes].astype(jnp.float32)
    pad[:, 3 : 3 + rows, 0:8, :] = jnp.zeros((chunks, rows, 8, LANES), jnp.float32)
    pad[:, 3 : 3 + rows, 8 + cols :, :] = jnp.zeros((chunks, rows, 8, LANES), jnp.float32)

    loads[1].wait()
    loads[2].wait()

    def own_part(c, carry):
        at = pl.ds(pl.multiple_of(c * LANES, LANES), LANES)
        acc = [jnp.broadcast_to(db[at].reshape(1, LANES), (cols, LANES)) for _ in range(rows)]
        for b in range(7):
            taps = [dw[a, b : b + 1, at] for a in range(7)]
            for r in range(3, 3 + rows):
                window = pad[c, r, b + 5 : b + 5 + cols, :]
                for a in range(7):
                    if 0 <= r - a < rows:
                        acc[r - a] = acc[r - a] + window * taps[a]
        for i in range(rows):
            conv[c, i] = acc[i]
        return carry

    lax.fori_loop(0, chunks, own_part, 0)

    loads[3].wait()
    q32[...] = queries[...].astype(jnp.float32)
    head = lane_ids(QROWS, width) // (width // NH)
    for at, step in enumerate(ORDER):
        other = near_peer(step)[0] if step else place
        some = q32[pl.ds(pl.multiple_of(other * QROWS, QROWS), QROWS), :]
        heads = [jnp.where(head == h, some, 0.0) for h in range(NH)]
        qbig[at * NH * QROWS : (at + 1) * NH * QROWS, :] = jnp.concatenate(heads, axis=0).astype(jnp.bfloat16)

    for side in SIDES:
        @pl.when(present(side))
        def _(side=side):
            pltpu.make_async_remote_copy(
                src_ref=landing[side],
                dst_ref=landing[side],
                send_sem=hs_sem.at[SIDES.index(side)],
                recv_sem=hr_sem.at[SIDES.index(side)],
                device_id=(row + side[0], col + side[1]),
                device_id_type=MESH,
            ).wait_recv()

    for c in range(chunks):
        lanes = slice(c * LANES, (c + 1) * LANES)
        for end, first in ((0, 0), (1, 3 + rows)):
            pad[c, first : first + 3, 8 : 8 + cols, :] = halo_rows[end, :, :, lanes].astype(jnp.float32)
            for side in range(2):
                corner = halo_corners[end * 2 + side, :, lanes].astype(jnp.float32).reshape(4, 8, LANES)
                start = 0 if side == 0 else 8 + cols
                pad[c, first : first + 3, start : start + 8, :] = corner[1:4] if end == 0 else corner[0:3]
        left_pad[c, :, 0:8, :] = halo_cols[0, :, lanes].astype(jnp.float32).reshape(rows, 8, LANES)
        right_pad[c, :, 8:16, :] = halo_cols[1, :, lanes].astype(jnp.float32).reshape(rows, 8, LANES)
    left_pad[:, :, 8:16, :] = jnp.zeros((chunks, rows, 8, LANES), jnp.float32)
    right_pad[:, :, 0:8, :] = jnp.zeros((chunks, rows, 8, LANES), jnp.float32)

    def border_part(c, carry):
        at = pl.ds(pl.multiple_of(c * LANES, LANES), LANES)
        acc = [conv[c, i] for i in range(rows)]
        low = [jnp.zeros((8, LANES), jnp.float32) for _ in range(rows)]
        high = [jnp.zeros((8, LANES), jnp.float32) for _ in range(rows)]
        for b in range(7):
            taps = [dw[a, b : b + 1, at] for a in range(7)]
            for r in list(range(3)) + list(range(3 + rows, 6 + rows)):
                window = pad[c, r, b + 5 : b + 5 + cols, :]
                for a in range(7):
                    if 0 <= r - a < rows:
                        acc[r - a] = acc[r - a] + window * taps[a]
            if b != 3:
                side, edge, start = (low, left_pad, b + 5) if b < 3 else (high, right_pad, b - 3)
                for r in range(3, 3 + rows):
                    window = edge[c, r - 3, start : start + 8, :]
                    for a in range(7):
                        if 0 <= r - a < rows:
                            side[r - a] = side[r - a] + window * taps[a]
        for i in range(rows):
            conv[c, i] = acc[i]
            conv[c, i, 0:8, :] = conv[c, i, 0:8, :] + low[i]
            conv[c, i, cols - 8 : cols, :] = conv[c, i, cols - 8 : cols, :] + high[i]
        return carry

    lax.fori_loop(0, chunks, border_part, 0)

    full = jnp.concatenate([conv[c].reshape(count, LANES) for c in range(chunks)], axis=1)
    center = jnp.mean(full, axis=-1, keepdims=True)
    off = full - center
    variance = jnp.mean(off * off, axis=-1, keepdims=True)
    for load in loads[4:11]:
        load.wait()
    normed = (
        off * lax.rsqrt(variance + 1e-06) * gain[...].reshape(1, width) + nbias[...].reshape(1, width)
    ).astype(jnp.bfloat16)

    hid = w1.shape[1]
    piece = 256
    shrunk = jnp.zeros((count, width), jnp.float32)
    starts = list(range(0, hid, piece))

    def expand(start):
        part = slice(start, start + piece)
        wide = jnp.dot(normed, w1[:, part], preferred_element_type=jnp.float32)
        return wide + b1[part].reshape(1, piece)

    expanded = expand(starts[0])
    for i, start in enumerate(starts):
        following = expand(starts[i + 1]) if i + 1 < len(starts) else None
        hidden = (0.5 * expanded * (1.0 + lax.erf(expanded * 0.5**0.5))).astype(jnp.bfloat16)
        shrunk = shrunk + jnp.dot(
            hidden, w2[start : start + piece, :], preferred_element_type=jnp.float32
        )
        expanded = following
    shrunk = shrunk + b2[...].reshape(1, width)
    inputs = feat[...].astype(jnp.float32).reshape(count, width)
    block = (inputs + scale[...].reshape(1, width) * shrunk).astype(jnp.bfloat16)
    block_ref[...] = block.reshape(rows, cols, width)

    for load in loads[11:]:
        load.wait()
    both = jnp.dot(block, wkv[...], preferred_element_type=jnp.float32).astype(jnp.bfloat16)
    keys, values = both[:, :width], both[:, width:]
    cell = lane_ids(1, count)
    tile = (cell // cols) // TILE * (cols // TILE) + (cell % cols) // TILE
    alive = jnp.zeros((1, count), jnp.int32)
    for i in range(rows // TILE):
        for j in range(cols // TILE):
            alive = jnp.where(tile == i * (cols // TILE) + j, tissue[i, j], alive)
    live = alive > 0
    lane = lane_ids(QROWS, LANES)
    copies_a = []
    per_call = GROUP // CALLS
    size = NH * QROWS
    for call in range(CALLS):
        scores = lax.dot_general(
            qbig[call * per_call * size : (call + 1) * per_call * size, :], keys,
            (((1,), (1,)), ((), ())), preferred_element_type=jnp.float32,
        ) * (width // NH) ** (-0.5)
        scores = jnp.where(live, scores, -1e30)
        peak = jnp.max(scores, axis=1, keepdims=True)
        weights = jnp.where(live, jnp.exp(scores - peak), 0.0)
        total = jnp.sum(weights, axis=1, keepdims=True)
        mixed = jnp.dot(weights.astype(jnp.bfloat16), values, preferred_element_type=jnp.float32)
        for i in range(per_call):
            at = call * per_call + i
            weighted = jnp.zeros((QROWS, width), jnp.float32)
            tail = jnp.zeros((QROWS, LANES), jnp.float32)
            for h in range(NH):
                own = slice(i * size + h * QROWS, i * size + (h + 1) * QROWS)
                weighted = jnp.where(head == h, mixed[own], weighted)
                tail = jnp.where(lane == h, peak[own], tail)
                tail = jnp.where(lane == NH + h, total[own], tail)
            step = ORDER[at]
            if step == 0:
                got_a[place, :, :width] = weighted
                got_a[place, :, width:] = tail
                continue
            msg[at, :, :width] = weighted
            msg[at, :, width:] = tail
            copies_a.append(pltpu.make_async_remote_copy(
                src_ref=msg.at[at],
                dst_ref=got_a.at[place],
                send_sem=as_sem.at[step],
                recv_sem=ar_sem.at[place],
                device_id=near_peer(step)[1],
                device_id_type=MESH,
            ))
            copies_a[-1].start()

    def arrival(dst, sem):
        return pltpu.make_async_remote_copy(
            src_ref=dst, dst_ref=dst, send_sem=as_sem.at[0], recv_sem=sem,
            device_id=near_peer(1)[1], device_id_type=MESH,
        )

    for step in range(1, GROUP):
        other = near_peer(step)[0]
        arrival(got_a.at[other], ar_sem.at[other]).wait_recv()
    weighted, tail = combine(got_a, GROUP, width)

    if n_far > 1:
        mine[:, :width] = weighted
        mine[:, width:] = tail
        copies_b = []
        for step in range(1, n_far):
            other, device = far_peer(step)
            copies_b.append(pltpu.make_async_remote_copy(
                src_ref=mine,
                dst_ref=got_b.at[far],
                send_sem=bs_sem.at[step],
                recv_sem=br_sem.at[far],
                device_id=device,
                device_id_type=MESH,
            ))
            copies_b[-1].start()
        got_b[far] = mine[...]
        for step in range(1, n_far):
            other = far_peer(step)[0]
            arrival(got_b.at[other], br_sem.at[other]).wait_recv()
        weighted, tail = combine(got_b, n_far, width)
    pooled[place] = weighted / spread(tail, NH, width)

    copies_c = []
    for step in ORDER[:-1]:
        other, device = near_peer(step)
        copies_c.append(pltpu.make_async_remote_copy(
            src_ref=pooled.at[place],
            dst_ref=pooled.at[place],
            send_sem=cs_sem.at[step],
            recv_sem=cr_sem.at[place],
            device_id=device,
            device_id_type=MESH,
        ))
        copies_c[-1].start()
    for step in range(1, GROUP):
        other = near_peer(step)[0]
        arrival(pooled.at[other], cr_sem.at[other]).wait_recv()
    result = pooled[...].reshape(NQ, width)
    pooled_ref[...] = result
    summed = jnp.sum(result, axis=0, keepdims=True)
    logits = jnp.sum(summed * cw[...], axis=1, keepdims=True)
    soft = jnp.maximum(logits, 0.0) + jnp.log1p(jnp.exp(-jnp.abs(logits)))
    n_lab = cw.shape[0]
    which = lax.broadcasted_iota(jnp.int32, (n_lab, 1), 0)
    truth = jnp.zeros((n_lab, 1), jnp.int32)
    for k in range(n_lab):
        truth = jnp.where(which == k, label[k], truth)
    loss_ref[0] = jnp.sum(soft - truth.astype(jnp.float32) * logits)

    for side in SIDES:
        @pl.when(present(side))
        def _(side=side):
            halo_copy(side).wait_send()
    for copy in copies_a:
        copy.wait_send()
    if n_far > 1:
        for copy in copies_b:
            copy.wait_send()
    for copy in copies_c:
        copy.wait_send()


def per_device(
    n_row, n_col,
    features, depth_weight, depth_bias, norm_gain, norm_bias, expand_weight, expand_bias,
    shrink_weight, shrink_bias, layer_scale, key_weight, value_weight, queries, class_weight,
    tissue, slide_label,
):
    rows, cols, width = features.shape
    hid = expand_weight.shape[1]
    chunks = width // LANES
    n_far = (n_row // GROUP_ROWS) * (n_col // GROUP_COLS)
    vmem = pl.BlockSpec(memory_space=pltpu.VMEM)
    smem = pl.BlockSpec(memory_space=pltpu.SMEM)
    hbm = pl.BlockSpec(memory_space=pltpu.HBM)
    wide = width + LANES
    f32, bf16 = jnp.float32, jnp.bfloat16
    dma = pltpu.SemaphoreType.DMA
    block, pooled, loss = pl.pallas_call(
        functools.partial(kernel, n_row, n_col),
        out_shape=(
            pltpu.VMEM((rows, cols, width), bf16),
            pltpu.VMEM((NQ, width), f32),
            jax.ShapeDtypeStruct((1,), f32),
        ),
        in_specs=[hbm] * 16,
        out_specs=(vmem, vmem, smem),
        scratch_shapes=[
            pltpu.VMEM((rows, cols, width), bf16),
            pltpu.VMEM(depth_weight.shape, f32),
            pltpu.VMEM((width,), f32),
            pltpu.VMEM((width,), f32),
            pltpu.VMEM((width,), f32),
            pltpu.VMEM((width, hid), bf16),
            pltpu.VMEM((hid,), f32),
            pltpu.VMEM((hid, width), bf16),
            pltpu.VMEM((width,), f32),
            pltpu.VMEM((width,), f32),
            pltpu.VMEM((width, 2 * width), bf16),
            pltpu.VMEM((NQ, width), bf16),
            pltpu.VMEM((class_weight.shape[1], width), f32),
            pltpu.SMEM(tissue.shape, jnp.int32),
            pltpu.SMEM(slide_label.shape, jnp.int32),
            pltpu.VMEM((NQ, width), f32),
            pltpu.VMEM((chunks, rows + 6, cols + 16, LANES), f32),
            pltpu.VMEM((chunks, rows, 16, LANES), f32),
            pltpu.VMEM((chunks, rows, 16, LANES), f32),
            pltpu.VMEM((chunks, rows, cols, LANES), f32),
            pltpu.VMEM((NH * NQ, width), bf16),
            pltpu.VMEM((rows * 8, width), bf16),
            pltpu.VMEM((rows * 8, width), bf16),
            pltpu.VMEM((2, 3, cols, width), bf16),
            pltpu.VMEM((2, rows * 8, width), bf16),
            pltpu.VMEM((4, 32, width), bf16),
            pltpu.VMEM((GROUP, QROWS, wide), f32),
            pltpu.VMEM((GROUP, QROWS, wide), f32),
            pltpu.VMEM((n_far, QROWS, wide), f32),
            pltpu.VMEM((QROWS, wide), f32),
            pltpu.VMEM((GROUP, QROWS, width), f32),
            dma((16,)),
            dma((8,)),
            dma((8,)),
            dma((GROUP,)),
            dma((GROUP,)),
            dma((n_far,)),
            dma((n_far,)),
            dma((GROUP,)),
            dma((GROUP,)),
        ],
        compiler_params=pltpu.CompilerParams(
            collective_id=0, has_side_effects=True, vmem_limit_bytes=63 * 1024 * 1024
        ),
    )(
        features, depth_weight, depth_bias, norm_gain, norm_bias, expand_weight, expand_bias,
        shrink_weight, shrink_bias, layer_scale, key_weight, value_weight, queries, class_weight.T,
        tissue, slide_label,
    )
    return block, pooled, loss


def solution(mesh):
    everywhere = P()
    cells = P("row", "col", None)
    placed = (cells,) + (everywhere,) * 13 + (P("row", "col"), everywhere)
    return jax.shard_map(
        functools.partial(per_device, mesh.shape["row"], mesh.shape["col"]),
        mesh=mesh,
        in_specs=placed,
        out_specs=(cells, everywhere, everywhere),
        check_vma=False,
    )
```

```python
import functools

import jax
import jax.numpy as jnp
from jax import lax
from jax.experimental import pallas as pl
from jax.experimental.pallas import tpu as pltpu
from jax.sharding import PartitionSpec as P

NH = 8
NQ = 64
TILE = 8
LANES = 128
GROUP_ROWS, GROUP_COLS = 4, 2
GROUP = GROUP_ROWS * GROUP_COLS
QROWS = NQ // GROUP
ORDER = (7, 5, 6, 4, 3, 1, 2, 0)
CALLS = 1
MESH = pl.DeviceIdType.MESH
SIDES = [(-1, 0), (1, 0), (0, -1), (0, 1), (-1, -1), (-1, 1), (1, -1), (1, 1)]


def lane_ids(rows, width):
    return lax.broadcasted_iota(jnp.int32, (rows, width), 1)


def spread(cols, first, width):
    rows = cols.shape[0]
    head = lane_ids(rows, width) // (width // NH)
    out = jnp.zeros((rows, width), jnp.float32)
    for h in range(NH):
        out = jnp.where(head == h, cols[:, first + h : first + h + 1], out)
    return out


def combine(ref, count, width):
    tails = [ref[s, :, width:] for s in range(count)]
    peak = functools.reduce(jnp.maximum, tails)
    weighted = jnp.zeros((QROWS, width), jnp.float32)
    total = jnp.zeros((QROWS, LANES), jnp.float32)
    for s in range(count):
        factor = jnp.exp(tails[s] - peak)
        total = total + pltpu.roll(factor, NH, 1) * tails[s]
        weighted = weighted + ref[s, :, :width] * spread(factor, 0, width)
    return weighted, jnp.where(lane_ids(QROWS, LANES) < NH, peak, total)


def kernel(
    n_row, n_col,
    feat_hbm, dw_hbm, db_hbm, gain_hbm, nbias_hbm, w1_hbm, b1_hbm, w2_hbm, b2_hbm, scale_hbm,
    wk_hbm, wv_hbm, queries_hbm, cw_hbm, tissue_hbm, label_hbm,
    block_ref, pooled_ref, loss_ref,
    feat, dw, db, gain, nbias, w1, b1, w2, b2, scale, wkv, queries, cw, tissue, label, q32, pad, left_pad, right_pad, conv, qbig,
    stage_l, stage_r, halo_rows, halo_cols, halo_corners, msg, got_a, got_b, mine, pooled,
    w_sem, hs_sem, hr_sem, as_sem, ar_sem, bs_sem, br_sem, cs_sem, cr_sem,
):
    rows, cols, width = feat_hbm.shape
    count = rows * cols
    chunks = width // LANES
    row, col = lax.axis_index("row"), lax.axis_index("col")

    sources = (
        (feat_hbm, feat), (dw_hbm, dw), (db_hbm, db), (queries_hbm, queries), (gain_hbm, gain),
        (nbias_hbm, nbias), (w1_hbm, w1), (b1_hbm, b1), (w2_hbm, w2), (b2_hbm, b2),
        (scale_hbm, scale), (wk_hbm, wkv.at[:, pl.ds(0, width)]),
        (wv_hbm, wkv.at[:, pl.ds(width, width)]), (cw_hbm, cw), (tissue_hbm, tissue),
        (label_hbm, label),
    )
    loads = [pltpu.make_async_copy(src, dst, w_sem.at[i]) for i, (src, dst) in enumerate(sources)]
    loads[0].start()

    base_row, base_col = (row // GROUP_ROWS) * GROUP_ROWS, (col // GROUP_COLS) * GROUP_COLS
    place = (row - base_row) * GROUP_COLS + (col - base_col)
    over = n_col // GROUP_COLS
    n_far = (n_row // GROUP_ROWS) * over
    far = (row // GROUP_ROWS) * over + col // GROUP_COLS

    def near_peer(step):
        other = (
            (place // 4 + step // 4) % 2 * 4
            + (place // 2 + step // 2) % 2 * 2
            + (place + step) % 2
        )
        return other, (base_row + other // GROUP_COLS, base_col + other % GROUP_COLS)

    def far_peer(step):
        other = (far + step) % n_far
        return other, (
            (other // over) * GROUP_ROWS + place // GROUP_COLS,
            (other % over) * GROUP_COLS + place % GROUP_COLS,
        )

    def present(side):
        dr, dc = side
        ok = None
        for delta, at, size in ((dr, row, n_row), (dc, col, n_col)):
            if delta:
                here = at > 0 if delta < 0 else at < size - 1
                ok = here if ok is None else jnp.logical_and(ok, here)
        return ok

    barrier = pltpu.get_barrier_semaphore()
    for side in SIDES:
        @pl.when(present(side))
        def _(side=side):
            pl.semaphore_signal(
                barrier, inc=1, device_id=(row + side[0], col + side[1]), device_id_type=MESH
            )
    for step in range(1, GROUP):
        pl.semaphore_signal(barrier, inc=1, device_id=near_peer(step)[1], device_id_type=MESH)
    for step in range(1, n_far):
        pl.semaphore_signal(barrier, inc=1, device_id=far_peer(step)[1], device_id_type=MESH)

    for load in loads[1:]:
        load.start()
    loads[0].wait()
    stage_l[...] = feat[:, 0:8, :].astype(jnp.float32).reshape(rows * 8, width).astype(jnp.bfloat16)
    stage_r[...] = (
        feat[:, cols - 8 : cols, :].astype(jnp.float32).reshape(rows * 8, width).astype(jnp.bfloat16)
    )

    landing = {
        (-1, 0): halo_rows.at[0], (1, 0): halo_rows.at[1],
        (0, -1): halo_cols.at[0], (0, 1): halo_cols.at[1],
        (-1, -1): halo_corners.at[0], (-1, 1): halo_corners.at[1],
        (1, -1): halo_corners.at[2], (1, 1): halo_corners.at[3],
    }

    def halo_copy(side):
        dr, dc = side
        if dc == 0:
            src = feat.at[pl.ds(0, 3)] if dr < 0 else feat.at[pl.ds(rows - 3, 3)]
        else:
            src = stage_l if dc < 0 else stage_r
            if dr:
                src = src.at[pl.ds(0 if dr < 0 else rows * 8 - 32, 32)]
        return pltpu.make_async_remote_copy(
            src_ref=src,
            dst_ref=landing[(-dr, -dc)],
            send_sem=hs_sem.at[SIDES.index(side)],
            recv_sem=hr_sem.at[SIDES.index((-dr, -dc))],
            device_id=(row + dr, col + dc),
            device_id_type=MESH,
        )

    greeted = jnp.int32(GROUP - 1 + n_far - 1)
    for side in SIDES:
        greeted = greeted + present(side).astype(jnp.int32)
    pl.semaphore_wait(barrier, greeted)
    for side in SIDES:
        @pl.when(present(side))
        def _(side=side):
            halo_copy(side).start()

        @pl.when(jnp.logical_not(present(side)))
        def _(side=side):
            landing[side][...] = jnp.zeros(landing[side].shape, jnp.bfloat16)

    for c in range(chunks):
        lanes = slice(c * LANES, (c + 1) * LANES)
        pad[c, 3 : 3 + rows, 8 : 8 + cols, :] = feat[:, :, lanes].astype(jnp.float32)
    pad[:, 3 : 3 + rows, 0:8, :] = jnp.zeros((chunks, rows, 8, LANES), jnp.float32)
    pad[:, 3 : 3 + rows, 8 + cols :, :] = jnp.zeros((chunks, rows, 8, LANES), jnp.float32)

    loads[1].wait()
    loads[2].wait()

    def own_part(c, carry):
        at = pl.ds(pl.multiple_of(c * LANES, LANES), LANES)
        acc = [jnp.broadcast_to(db[at].reshape(1, LANES), (cols, LANES)) for _ in range(rows)]
        for b in range(7):
            taps = [dw[a, b : b + 1, at] for a in range(7)]
            for r in range(3, 3 + rows):
                window = pad[c, r, b + 5 : b + 5 + cols, :]
                for a in range(7):
                    if 0 <= r - a < rows:
                        acc[r - a] = acc[r - a] + window * taps[a]
        for i in range(rows):
            conv[c, i] = acc[i]
        return carry

    lax.fori_loop(0, chunks, own_part, 0)

    loads[3].wait()
    q32[...] = queries[...].astype(jnp.float32)
    head = lane_ids(QROWS, width) // (width // NH)
    for at, step in enumerate(ORDER):
        other = near_peer(step)[0] if step else place
        some = q32[pl.ds(pl.multiple_of(other * QROWS, QROWS), QROWS), :]
        heads = [jnp.where(head == h, some, 0.0) for h in range(NH)]
        qbig[at * NH * QROWS : (at + 1) * NH * QROWS, :] = jnp.concatenate(heads, axis=0).astype(jnp.bfloat16)

    for side in SIDES:
        @pl.when(present(side))
        def _(side=side):
            pltpu.make_async_remote_copy(
                src_ref=landing[side],
                dst_ref=landing[side],
                send_sem=hs_sem.at[SIDES.index(side)],
                recv_sem=hr_sem.at[SIDES.index(side)],
                device_id=(row + side[0], col + side[1]),
                device_id_type=MESH,
            ).wait_recv()

    for c in range(chunks):
        lanes = slice(c * LANES, (c + 1) * LANES)
        for end, first in ((0, 0), (1, 3 + rows)):
            pad[c, first : first + 3, 8 : 8 + cols, :] = halo_rows[end, :, :, lanes].astype(jnp.float32)
            for side in range(2):
                corner = halo_corners[end * 2 + side, :, lanes].astype(jnp.float32).reshape(4, 8, LANES)
                start = 0 if side == 0 else 8 + cols
                pad[c, first : first + 3, start : start + 8, :] = corner[1:4] if end == 0 else corner[0:3]
        left_pad[c, :, 0:8, :] = halo_cols[0, :, lanes].astype(jnp.float32).reshape(rows, 8, LANES)
        right_pad[c, :, 8:16, :] = halo_cols[1, :, lanes].astype(jnp.float32).reshape(rows, 8, LANES)
    left_pad[:, :, 8:16, :] = jnp.zeros((chunks, rows, 8, LANES), jnp.float32)
    right_pad[:, :, 0:8, :] = jnp.zeros((chunks, rows, 8, LANES), jnp.float32)

    def border_part(c, carry):
        at = pl.ds(pl.multiple_of(c * LANES, LANES), LANES)
        acc = [conv[c, i] for i in range(rows)]
        low = [jnp.zeros((8, LANES), jnp.float32) for _ in range(rows)]
        high = [jnp.zeros((8, LANES), jnp.float32) for _ in range(rows)]
        for b in range(7):
            taps = [dw[a, b : b + 1, at] for a in range(7)]
            for r in list(range(3)) + list(range(3 + rows, 6 + rows)):
                window = pad[c, r, b + 5 : b + 5 + cols, :]
                for a in range(7):
                    if 0 <= r - a < rows:
                        acc[r - a] = acc[r - a] + window * taps[a]
            if b != 3:
                side, edge, start = (low, left_pad, b + 5) if b < 3 else (high, right_pad, b - 3)
                for r in range(3, 3 + rows):
                    window = edge[c, r - 3, start : start + 8, :]
                    for a in range(7):
                        if 0 <= r - a < rows:
                            side[r - a] = side[r - a] + window * taps[a]
        for i in range(rows):
            conv[c, i] = acc[i]
            conv[c, i, 0:8, :] = conv[c, i, 0:8, :] + low[i]
            conv[c, i, cols - 8 : cols, :] = conv[c, i, cols - 8 : cols, :] + high[i]
        return carry

    lax.fori_loop(0, chunks, border_part, 0)

    full = jnp.concatenate([conv[c].reshape(count, LANES) for c in range(chunks)], axis=1)
    center = jnp.mean(full, axis=-1, keepdims=True)
    off = full - center
    variance = jnp.mean(off * off, axis=-1, keepdims=True)
    for load in loads[4:11]:
        load.wait()
    normed = (
        off * lax.rsqrt(variance + 1e-06) * gain[...].reshape(1, width) + nbias[...].reshape(1, width)
    ).astype(jnp.bfloat16)

    hid = w1.shape[1]
    piece = 256
    hiddens = []
    starts = list(range(0, hid, piece))

    def expand(start):
        part = slice(start, start + piece)
        wide = jnp.dot(normed, w1[:, part], preferred_element_type=jnp.float32)
        return wide + b1[part].reshape(1, piece)

    expanded = expand(starts[0])
    for i, start in enumerate(starts):
        following = expand(starts[i + 1]) if i + 1 < len(starts) else None
        hidden = (0.5 * expanded * (1.0 + lax.erf(expanded * 0.5**0.5))).astype(jnp.bfloat16)
        hiddens.append(hidden)
        expanded = following
    shrunk = jnp.dot(jnp.concatenate(hiddens, axis=1), w2[...], preferred_element_type=jnp.float32)
    shrunk = shrunk + b2[...].reshape(1, width)
    inputs = feat[...].astype(jnp.float32).reshape(count, width)
    block = (inputs + scale[...].reshape(1, width) * shrunk).astype(jnp.bfloat16)
    block_ref[...] = block.reshape(rows, cols, width)

    for load in loads[11:]:
        load.wait()
    both = jnp.dot(block, wkv[...], preferred_element_type=jnp.float32).astype(jnp.bfloat16)
    keys, values = both[:, :width], both[:, width:]
    cell = lane_ids(1, count)
    tile = (cell // cols) // TILE * (cols // TILE) + (cell % cols) // TILE
    alive = jnp.zeros((1, count), jnp.int32)
    for i in range(rows // TILE):
        for j in range(cols // TILE):
            alive = jnp.where(tile == i * (cols // TILE) + j, tissue[i, j], alive)
    live = alive > 0
    lane = lane_ids(QROWS, LANES)
    copies_a = []
    per_call = GROUP // CALLS
    size = NH * QROWS
    for call in range(CALLS):
        scores = lax.dot_general(
            qbig[call * per_call * size : (call + 1) * per_call * size, :], keys,
            (((1,), (1,)), ((), ())), preferred_element_type=jnp.float32,
        ) * (width // NH) ** (-0.5)
        scores = jnp.where(live, scores, -1e30)
        peak = jnp.max(scores, axis=1, keepdims=True)
        weights = jnp.where(live, jnp.exp(scores - peak), 0.0)
        total = jnp.sum(weights, axis=1, keepdims=True)
        mixed = jnp.dot(weights.astype(jnp.bfloat16), values, preferred_element_type=jnp.float32)
        for i in range(per_call):
            at = call * per_call + i
            weighted = jnp.zeros((QROWS, width), jnp.float32)
            tail = jnp.zeros((QROWS, LANES), jnp.float32)
            for h in range(NH):
                own = slice(i * size + h * QROWS, i * size + (h + 1) * QROWS)
                weighted = jnp.where(head == h, mixed[own], weighted)
                tail = jnp.where(lane == h, peak[own], tail)
                tail = jnp.where(lane == NH + h, total[own], tail)
            step = ORDER[at]
            if step == 0:
                got_a[place, :, :width] = weighted
                got_a[place, :, width:] = tail
                continue
            msg[at, :, :width] = weighted
            msg[at, :, width:] = tail
            copies_a.append(pltpu.make_async_remote_copy(
                src_ref=msg.at[at],
                dst_ref=got_a.at[place],
                send_sem=as_sem.at[step],
                recv_sem=ar_sem.at[place],
                device_id=near_peer(step)[1],
                device_id_type=MESH,
            ))
            copies_a[-1].start()

    def arrival(dst, sem):
        return pltpu.make_async_remote_copy(
            src_ref=dst, dst_ref=dst, send_sem=as_sem.at[0], recv_sem=sem,
            device_id=near_peer(1)[1], device_id_type=MESH,
        )

    for step in range(1, GROUP):
        other = near_peer(step)[0]
        arrival(got_a.at[other], ar_sem.at[other]).wait_recv()
    weighted, tail = combine(got_a, GROUP, width)

    if n_far > 1:
        mine[:, :width] = weighted
        mine[:, width:] = tail
        copies_b = []
        for step in range(1, n_far):
            other, device = far_peer(step)
            copies_b.append(pltpu.make_async_remote_copy(
                src_ref=mine,
                dst_ref=got_b.at[far],
                send_sem=bs_sem.at[step],
                recv_sem=br_sem.at[far],
                device_id=device,
                device_id_type=MESH,
            ))
            copies_b[-1].start()
        got_b[far] = mine[...]
        for step in range(1, n_far):
            other = far_peer(step)[0]
            arrival(got_b.at[other], br_sem.at[other]).wait_recv()
        weighted, tail = combine(got_b, n_far, width)
    pooled[place] = weighted / spread(tail, NH, width)

    copies_c = []
    for step in ORDER[:-1]:
        other, device = near_peer(step)
        copies_c.append(pltpu.make_async_remote_copy(
            src_ref=pooled.at[place],
            dst_ref=pooled.at[place],
            send_sem=cs_sem.at[step],
            recv_sem=cr_sem.at[place],
            device_id=device,
            device_id_type=MESH,
        ))
        copies_c[-1].start()
    for step in range(1, GROUP):
        other = near_peer(step)[0]
        arrival(pooled.at[other], cr_sem.at[other]).wait_recv()
    result = pooled[...].reshape(NQ, width)
    pooled_ref[...] = result
    summed = jnp.sum(result, axis=0, keepdims=True)
    logits = jnp.sum(summed * cw[...], axis=1, keepdims=True)
    soft = jnp.maximum(logits, 0.0) + jnp.log1p(jnp.exp(-jnp.abs(logits)))
    n_lab = cw.shape[0]
    which = lax.broadcasted_iota(jnp.int32, (n_lab, 1), 0)
    truth = jnp.zeros((n_lab, 1), jnp.int32)
    for k in range(n_lab):
        truth = jnp.where(which == k, label[k], truth)
    loss_ref[0] = jnp.sum(soft - truth.astype(jnp.float32) * logits)

    for side in SIDES:
        @pl.when(present(side))
        def _(side=side):
            halo_copy(side).wait_send()
    for copy in copies_a:
        copy.wait_send()
    if n_far > 1:
        for copy in copies_b:
            copy.wait_send()
    for copy in copies_c:
        copy.wait_send()


def per_device(
    n_row, n_col,
    features, depth_weight, depth_bias, norm_gain, norm_bias, expand_weight, expand_bias,
    shrink_weight, shrink_bias, layer_scale, key_weight, value_weight, queries, class_weight,
    tissue, slide_label,
):
    rows, cols, width = features.shape
    hid = expand_weight.shape[1]
    chunks = width // LANES
    n_far = (n_row // GROUP_ROWS) * (n_col // GROUP_COLS)
    vmem = pl.BlockSpec(memory_space=pltpu.VMEM)
    smem = pl.BlockSpec(memory_space=pltpu.SMEM)
    hbm = pl.BlockSpec(memory_space=pltpu.HBM)
    wide = width + LANES
    f32, bf16 = jnp.float32, jnp.bfloat16
    dma = pltpu.SemaphoreType.DMA
    block, pooled, loss = pl.pallas_call(
        functools.partial(kernel, n_row, n_col),
        out_shape=(
            pltpu.VMEM((rows, cols, width), bf16),
            pltpu.VMEM((NQ, width), f32),
            jax.ShapeDtypeStruct((1,), f32),
        ),
        in_specs=[hbm] * 16,
        out_specs=(vmem, vmem, smem),
        scratch_shapes=[
            pltpu.VMEM((rows, cols, width), bf16),
            pltpu.VMEM(depth_weight.shape, f32),
            pltpu.VMEM((width,), f32),
            pltpu.VMEM((width,), f32),
            pltpu.VMEM((width,), f32),
            pltpu.VMEM((width, hid), bf16),
            pltpu.VMEM((hid,), f32),
            pltpu.VMEM((hid, width), bf16),
            pltpu.VMEM((width,), f32),
            pltpu.VMEM((width,), f32),
            pltpu.VMEM((width, 2 * width), bf16),
            pltpu.VMEM((NQ, width), bf16),
            pltpu.VMEM((class_weight.shape[1], width), f32),
            pltpu.SMEM(tissue.shape, jnp.int32),
            pltpu.SMEM(slide_label.shape, jnp.int32),
            pltpu.VMEM((NQ, width), f32),
            pltpu.VMEM((chunks, rows + 6, cols + 16, LANES), f32),
            pltpu.VMEM((chunks, rows, 16, LANES), f32),
            pltpu.VMEM((chunks, rows, 16, LANES), f32),
            pltpu.VMEM((chunks, rows, cols, LANES), f32),
            pltpu.VMEM((NH * NQ, width), bf16),
            pltpu.VMEM((rows * 8, width), bf16),
            pltpu.VMEM((rows * 8, width), bf16),
            pltpu.VMEM((2, 3, cols, width), bf16),
            pltpu.VMEM((2, rows * 8, width), bf16),
            pltpu.VMEM((4, 32, width), bf16),
            pltpu.VMEM((GROUP, QROWS, wide), f32),
            pltpu.VMEM((GROUP, QROWS, wide), f32),
            pltpu.VMEM((n_far, QROWS, wide), f32),
            pltpu.VMEM((QROWS, wide), f32),
            pltpu.VMEM((GROUP, QROWS, width), f32),
            dma((16,)),
            dma((8,)),
            dma((8,)),
            dma((GROUP,)),
            dma((GROUP,)),
            dma((n_far,)),
            dma((n_far,)),
            dma((GROUP,)),
            dma((GROUP,)),
        ],
        compiler_params=pltpu.CompilerParams(
            collective_id=0, has_side_effects=True, vmem_limit_bytes=63 * 1024 * 1024
        ),
    )(
        features, depth_weight, depth_bias, norm_gain, norm_bias, expand_weight, expand_bias,
        shrink_weight, shrink_bias, layer_scale, key_weight, value_weight, queries, class_weight.T,
        tissue, slide_label,
    )
    return block, pooled, loss


def solution(mesh):
    everywhere = P()
    cells = P("row", "col", None)
    placed = (cells,) + (everywhere,) * 13 + (P("row", "col"), everywhere)
    return jax.shard_map(
        functools.partial(per_device, mesh.shape["row"], mesh.shape["col"]),
        mesh=mesh,
        in_specs=placed,
        out_specs=(cells, everywhere, everywhere),
        check_vma=False,
    )
```
